32 devices in a mesh: stream: 8 (over z, y), pitch: 4 (over x, core).
Axes of the slice: x: 2, y: 2, z: 4, core: 2. Of those that a mesh axis runs over, the one named last changes fastest.
Arguments:
- velocity: float32 [64, 64, 1024], P('stream', 'pitch'), may hold values from -6 to 6
- eddy_visc: float32 [64, 64, 1024], P('stream', 'pitch'), may hold values from 0.02 to 0.3
- stream_op: float32 [64, 64], replicated, may hold values from -0.75 to 0.75
- inlet_col: float32 [64], replicated, may hold values from -5 to 5
- planes: float32 [8, 64, 1024], P('stream', 'pitch'), may hold values from -6 to 6
- record: int32 [4], replicated, may hold values from 0 to 7
- convection: float32 [64], P('pitch'), may hold values from 0.5 to 2
- span_speed: float32 [64], P('pitch'), may hold values from 0.5 to 2.5
- span_filter: float32 [512], replicated, may hold values from 0.25 to 1
Outputs:
- advanced: float32 [64, 64, 1024], P('stream', 'pitch')
The draws below stay inside these ranges and needn't reach their ends.
All inputs are finite; a program needn't handle non-finite values.
Results may differ from the reference program's by a relative error of at most 0.00008.
Values sent between devices are 32-bit elements; how exact they have to be, the bound alone decides.
A program may use at most 128 MiB of HBM per device.

```python
import math
import jax
import jax.numpy as jnp
from jax import lax

NZ = 1024
SECTIONS = 4
NX = 64
NY = 64
RECORDS = 8


def with_ends(drawn, stream_key, least, largest):
    index_at = [jax.random.randint(jax.random.fold_in(stream_key, axis), (), 0, length) for axis, length in enumerate(drawn.shape)]
    longest = drawn.shape.index(max(drawn.shape))
    next_to = index_at[:longest] + [(index_at[longest] + 1) % drawn.shape[longest]] + index_at[longest + 1:]
    return drawn.at[tuple(index_at)].set(least).at[tuple(next_to)].set(largest)


def levels(own_key, extent, cuts, low, top_value):
    gain, own = 1.0, jax.random.fold_in(own_key, 6)
    for position, parts in cuts:
        steps = jnp.exp(jax.random.uniform(jax.random.fold_in(own, position), (parts,), jnp.float32, low / len(cuts), top_value / len(cuts)))
        gain = gain * jnp.repeat(steps, extent[position] // parts).reshape([-1 if axis == position else 1 for axis in range(len(extent))])
    return gain


def normal_values(key, dims, deviation, bound, pieces=(), dtype=jnp.bfloat16):
    gain = levels(key, dims, pieces, -0.22, 0.18) if pieces else 1.0
    drawn = jax.random.normal(key, dims, jnp.float32) * deviation * gain
    return jnp.minimum(jnp.maximum(drawn, -bound), bound).astype(dtype)


def setup_inputs(seed: int = 0) -> dict:
    splits = jax.random.split(jax.random.key(seed), 10)
    velocity = normal_values(splits[0], (NX, NY, NZ), 1.0, 6.0, ((0, 8), (1, 4)), jnp.float32)
    eddy_visc = jnp.clip(jnp.exp(math.log(0.3) - 2.7080503 * jax.random.uniform(splits[1], (NX, NY, NZ), jnp.float32) ** levels(splits[1], (NX, NY, NZ), ((0, 8), (1, 4)), -0.2, 0.2)), 0.02, 0.3)
    stream_op = normal_values(splits[2], (NX, NX), NX ** -0.5, 0.75, (), jnp.float32)
    inlet_col = normal_values(splits[3], (NX,), 1.0, 5.0, (), jnp.float32)
    planes = normal_values(splits[4], (RECORDS, NY, NZ), 1.0, 6.0, ((0, 8), (1, 4)), jnp.float32)
    record = with_ends(jax.random.randint(splits[5], (SECTIONS,), 0, RECORDS), jax.random.fold_in(splits[5], 1), 0, RECORDS - 1).astype(jnp.int32)
    convection = jnp.clip(jnp.exp(math.log(2.0) - 1.3862944 * jax.random.uniform(splits[6], (NY,), jnp.float32) ** levels(splits[6], (NY,), ((0, 4),), -0.2, 0.2)), 0.5, 2.0)
    span_speed = jnp.clip(0.5 + 2.0 * jax.random.uniform(splits[7], (NY,), jnp.float32) ** levels(splits[7], (NY,), ((0, 4),), -0.2, 0.2), 0.5, 2.5)
    span_filter = jnp.clip(jax.random.uniform(splits[8], (NZ // 2,), jnp.float32, 0.25, 1.0), 0.25, 1.0)
    return dict(velocity=velocity, eddy_visc=eddy_visc, stream_op=stream_op, inlet_col=inlet_col, planes=planes, record=record, convection=convection, span_speed=span_speed, span_filter=span_filter)


time_step = 0.25


def pitch_second(field):
    return (-jnp.roll(field, 2, axis=1) + 16.0 * jnp.roll(field, 1, axis=1) - 30.0 * field
            + 16.0 * jnp.roll(field, -1, axis=1) - jnp.roll(field, -2, axis=1)) / 12.0


def span_term(field, span_filter):
    half = NZ // 2
    modes = jnp.arange(half).astype(jnp.float32)
    gains = jnp.concatenate([span_filter * modes / half, jnp.zeros((1,), jnp.float32)])
    spectrum = jnp.fft.rfft(field, axis=2)
    return jnp.fft.irfft(1j * gains[None, None, :] * spectrum, n=NZ, axis=2)


def section_rate(state, inlet, eddy_visc, stream_op, inlet_col, convection, span_speed, span_filter):
    stream_deriv = jnp.einsum("ab,byz->ayz", stream_op, state, precision=lax.Precision.HIGHEST)
    stream_deriv = stream_deriv + inlet_col[:, None, None] * inlet[None, :, :]
    return (-(convection[None, :, None] + state) * stream_deriv
            - span_speed[None, :, None] * span_term(state, span_filter)
            + eddy_visc * pitch_second(state))


def reference(velocity, eddy_visc, stream_op, inlet_col, planes, record, convection, span_speed, span_filter):
    def rate(state, section):
        inlet = planes[record[section]]
        return section_rate(state, inlet, eddy_visc, stream_op, inlet_col, convection, span_speed, span_filter)

    first = rate(velocity, 0)
    second = rate(velocity + 0.5 * time_step * first, 1)
    third = rate(velocity + 0.5 * time_step * second, 2)
    fourth = rate(velocity + time_step * third, 3)
    return velocity + (time_step / 6.0) * (first + 2.0 * second + 2.0 * third + fourth)
```

```python
import math

import jax
import jax.numpy as jnp
import numpy as np
from jax import lax
from jax.experimental import pallas as pl
from jax.experimental.pallas import tpu as pltpu
from jax.sharding import PartitionSpec as P

time_step = 0.25


def spread(shard, axis, root):
    mine = lax.axis_index(axis) == root
    return lax.psum(jnp.where(mine, shard, jnp.zeros_like(shard)), axis)


def with_halo(shard, sides, width):
    for axis, dim in sides:
        peers, length = (lax.axis_size(axis), shard.shape[dim])
        up = [(i, (i + 1) % peers) for i in range(peers)]
        down = [(j, i) for i, j in up]
        last = lax.slice_in_dim(shard, length - width, length, axis=dim)
        initial = lax.slice_in_dim(shard, 0, width, axis=dim)
        before = lax.ppermute(last, axis, up)
        after = lax.ppermute(initial, axis, down)
        shard = jnp.concatenate([before, shard, after], axis=dim)
    return shard


def pitch_second(padded):
    return (
        -padded[:, 0:-4]
        + 16.0 * padded[:, 1:-3]
        - 30.0 * padded[:, 2:-2]
        + 16.0 * padded[:, 3:-1]
        - padded[:, 4:]
    ) / 12.0


def shards(
    velocity, eddy_visc, stream_op, inlet_col, planes, record, convection, span_speed, span_filter
):
    cells_x, cells_y, span_len = velocity.shape
    stream_len = stream_op.shape[0]
    span_piece = span_len // lax.axis_size("stream")
    position = lax.axis_index("stream")
    half = span_len // 2
    rows_index = lax.iota(jnp.int32, span_len)[:, None]
    mode_index = lax.iota(jnp.int32, half)[None, :]
    angle = (rows_index * mode_index % span_len).astype(jnp.float32) * (2.0 * math.pi / span_len)
    table_dft = jnp.concatenate([jnp.cos(angle), jnp.sin(angle)], axis=1)
    gains = span_filter * lax.iota(jnp.float32, half) / half
    conv_rows = convection[None, :, None]
    span_rows = span_speed[None, :, None]

    def inlet_at(section):
        whole = spread(planes[0], "stream", record[section])
        return lax.dynamic_slice_in_dim(whole, position * span_piece, span_piece, 1)

    def span_part(state):
        flat = state.reshape(-1, span_len)
        coeffs = jnp.dot(
            flat, table_dft, precision=lax.Precision.HIGHEST, preferred_element_type=jnp.float32
        )
        mixed = jnp.concatenate([coeffs[:, half:] * gains, -coeffs[:, :half] * gains], axis=1)
        back = lax.dot_general(
            mixed,
            table_dft,
            (((1,), (1,)), ((), ())),
            precision=lax.Precision.HIGHEST,
            preferred_element_type=jnp.float32,
        )
        return (back * (2.0 / span_len)).reshape(state.shape)

    def section_rate(state, section):
        inlet_slice = inlet_at(section)
        pencil = lax.all_to_all(state, "stream", split_axis=2, concat_axis=0, tiled=True)
        stream_deriv = jnp.dot(
            stream_op,
            pencil.reshape(stream_len, -1),
            precision=lax.Precision.HIGHEST,
            preferred_element_type=jnp.float32,
        )
        stream_deriv = (
            stream_deriv.reshape(pencil.shape) + inlet_col[:, None, None] * inlet_slice[None, :, :]
        )
        returned = lax.all_to_all(stream_deriv, "stream", split_axis=0, concat_axis=2, tiled=True)
        padded = with_halo(state, (("pitch", 1),), 2)
        local_terms = -(conv_rows + state) * returned + eddy_visc * pitch_second(padded)
        return local_terms - span_rows * span_part(state)

    first = section_rate(velocity, 0)
    second = section_rate(velocity + 0.5 * time_step * first, 1)
    third = section_rate(velocity + 0.5 * time_step * second, 2)
    fourth = section_rate(velocity + time_step * third, 3)
    return velocity + time_step / 6.0 * (first + 2.0 * second + 2.0 * third + fourth)


CHUNK = 8
PAIR = 2
MESH_ID = pl.DeviceIdType.MESH


def place_of(rank):
    spot, turn = rank // 2, rank % 2
    plane, step = spot // 8, spot % 8
    along = step + plane * (7 - 2 * step)
    depth = along // 2
    core = (plane + depth // 2 + step + turn) % 2
    return 2 * depth + (along + 1) // 2 % 2, 2 * plane + core


def rank_of(stream, pitch):
    depth, side, plane, core = stream // 2, stream % 2, pitch // 2, pitch % 2
    along = 2 * depth + (side + depth) % 2
    step = along + plane * (7 - 2 * along)
    return 2 * (8 * plane + step) + (core + plane + depth // 2 + step) % 2


def halves(value):
    high = value.astype(jnp.bfloat16)
    return high, (value - high.astype(jnp.float32)).astype(jnp.bfloat16)


def mul(left, right):
    return jnp.dot(left, right, preferred_element_type=jnp.float32)


def ring_kernel(
    vel_hbm, eddy_hbm, op_hbm, col_hbm, plane_hbm, record_hbm, conv_hbm, speed_hbm, filter_hbm, table_hbm,
    out_ref,
    vel_ref, eddy_ref, op_ref, inlet_ref, plane_ref, record_ref, conv_ref, speed_ref, filter_ref, table_ref,
    in_sems, col_ref, rows_ref,
    vt, et, pt, state, eddy, inlets, row_vals, low, high, total, dx, sz, weights, op_cat,
    vel_send, vel_recv, eddy_send, eddy_recv, pl_send, pl_recv, row_send, row_recv,
    low_send, low_recv, high_send, high_recv, out_send, out_recv,
    eddy_via, eddy_via_recv, eddy_on, edge_send,
):
    me_s, me_p = lax.axis_index("stream"), lax.axis_index("pitch")
    me = rank_of(me_s, me_p)
    home = me // 8
    offset = me % 8
    above = place_of((me + 1) % 32)
    below = place_of((me + 31) % 32)
    partner = (me_s, me_p + 1 - 2 * (me_p % 2))
    core = me_p % 2
    upper = me_s // 4
    group_upper = (me_p + 1) // 2 % 2
    feeds = (me_s == 2) | (me_s == 4)
    relays = (me_s == 3) | (me_s == 5)
    feeds_in = feeds & (group_upper != upper)
    relays_in = relays & (group_upper == upper)
    crossing = group_upper != upper
    mirrored = (me_s + 2 * (1 - upper)) % 4
    first_vel = jnp.where(crossing & (mirrored < 2), 6, 2)
    first_eddy = jnp.where(crossing & (mirrored == 1), 6, 2)
    edge = 7 * (1 - core)
    edge_peer = place_of((8 * me_p + edge + 33 - 2 * core) % 32)
    ends_low, ends_high = me % 16 == 7, me % 16 == 8
    inner = (offset >= 2) & (offset <= 5)

    def arrival(i):
        turn = jnp.where(inner, 7 - i % 4, 4 + i % 4)
        return jnp.where(i < 4, 4 * upper + i % 4, jnp.where(upper == 1, (turn + 2) % 4, turn))

    loads = [
        pltpu.make_async_copy(source, target, in_sems.at[i])
        for i, (source, target) in enumerate(
            (
                (vel_hbm, vel_ref), (plane_hbm, plane_ref), (conv_hbm, conv_ref), (speed_hbm, speed_ref),
                (eddy_hbm, eddy_ref), (filter_hbm, filter_ref), (table_hbm, table_ref), (op_hbm, op_ref),
                (col_hbm, inlet_ref), (record_hbm, record_ref),
            )
        )
    ]
    for load in loads[:4]:
        load.start()

    barrier = pltpu.get_barrier_semaphore()

    @pl.loop(1, 32)
    def _(step):
        other = (me_s * 4 + me_p + step) % 32
        pl.semaphore_signal(barrier, inc=1, device_id=(other // 4, other % 4), device_id_type=MESH_ID)

    def rows8(index):
        return pl.ds(pl.multiple_of(index * CHUNK, CHUNK), CHUNK)

    def out_copy(src, dst, send, recv, device):
        return pltpu.make_async_remote_copy(
            src_ref=src, dst_ref=dst, send_sem=send, recv_sem=recv, device_id=device,
            device_id_type=MESH_ID,
        )

    def spread_copy(kind, j):
        src, dst, send, recv = {
            "vel": (vt, state.at[0], vel_send, vel_recv),
            "eddy": (et, eddy, eddy_send, eddy_recv),
            "plane": (pt, inlets, pl_send, pl_recv),
        }[kind]
        source = src.at[pl.ds(PAIR * j, PAIR)]
        target = dst.at[me_s] if kind == "plane" else dst.at[:, rows8(me_s)]
        rank = 8 * me_p + j
        return (
            rank,
            out_copy(source, target, send.at[j], recv.at[me_s], place_of(rank)),
            lambda: pltpu.make_async_copy(source, target, recv.at[me_s]),
        )

    def spread_start(kind, j):
        rank, remote, local = spread_copy(kind, j)

        via = feeds_in & (j >= 2) & (j <= 5) if kind == "eddy" else False

        @pl.when((rank != me) & jnp.logical_not(via))
        def _():
            remote.start()

        @pl.when(rank == me)
        def _():
            local().start()

        if kind == "eddy":

            @pl.when(via)
            def _():
                k = (j + 6) % 8
                out_copy(
                    et.at[pl.ds(PAIR * j, PAIR)], eddy_via.at[k], eddy_send.at[j], eddy_via_recv.at[k],
                    (me_s + 1, me_p + 1 - 2 * core),
                ).start()

    def forward_eddy(k):
        source = (me_s + 7) % 8
        return (
            pltpu.make_async_copy(eddy_via.at[k], eddy_via.at[k], eddy_via_recv.at[k]),
            out_copy(
                eddy_via.at[k], eddy.at[:, rows8(source)], eddy_on.at[k], eddy_recv.at[source],
                place_of(8 * (me_p + 1 - 2 * core) + 2 + k),
            ),
        )

    def edge_copy(to_low):
        dst, recv = (low, low_recv) if to_low else (high, high_recv)
        return out_copy(
            vt.at[pl.ds(PAIR * edge, PAIR)], dst.at[0, :, rows8(me_s)], edge_send, recv.at[0, me_s],
            edge_peer,
        )

    def edge_start(j):
        @pl.when(crossing & (j == edge) & (core == 0))
        def _():
            edge_copy(True).start()

        @pl.when(crossing & (j == edge) & (core == 1))
        def _():
            edge_copy(False).start()

    def low_sends(n, c):
        return jnp.logical_not(ends_low & (c // 4 != upper)) if n == 0 else True

    def high_sends(n, c):
        return jnp.logical_not(ends_high & (c // 4 != upper)) if n == 0 else True

    def spread_sent(kind):
        @pl.loop(0, 8)
        def _(j):
            rank, remote, _local = spread_copy(kind, j)

            @pl.when(rank != me)
            def _():
                remote.wait_send()

    def spread_arrived(kind, s):
        src, dst, send, recv = {
            "vel": (vt, state.at[0], vel_send, vel_recv),
            "eddy": (et, eddy, eddy_send, eddy_recv),
            "plane": (pt, inlets, pl_send, pl_recv),
        }[kind]
        target = dst.at[s] if kind == "plane" else dst.at[:, rows8(s)]
        pltpu.make_async_copy(src.at[pl.ds(0, PAIR)], target, recv.at[s]).wait()

    def low_copy(n, c):
        return out_copy(
            state.at[n, :, rows8(c)], low.at[n, :, rows8(c)], low_send.at[n, c], low_recv.at[n, c], above
        )

    def high_copy(n, c):
        return out_copy(
            state.at[n, :, rows8(c)], high.at[n, :, rows8(c)], high_send.at[n, c], high_recv.at[n, c],
            below,
        )

    def result_copy(s):
        source = state.at[4, :, rows8(s)]
        target = out_ref.at[pl.ds(PAIR * offset, PAIR)]
        return (
            out_copy(source, target, out_send.at[s], out_recv.at[offset], (s, home)),
            lambda: pltpu.make_async_copy(source, target, out_recv.at[offset]),
        )

    loads[0].wait()
    for load in loads[4:]:
        load.start()

    pl.semaphore_wait(barrier, 31)

    @pl.loop(0, 8)
    def _(i):
        j = (i + first_vel) % 8
        for y in range(PAIR):
            vt[PAIR * j + y] = jnp.squeeze(vel_ref[:, pl.ds(PAIR * j + y, 1), :], axis=1)
        spread_start("vel", j)
        edge_start(j)

    def column_of(row):
        count = row.shape[1]
        own = lax.broadcasted_iota(jnp.int32, (count, count), 0) == lax.broadcasted_iota(
            jnp.int32, (count, count), 1
        )
        picked = jnp.sum(jnp.where(own, jnp.broadcast_to(row, (count, count)), 0.0), axis=1, keepdims=True)
        return jnp.broadcast_to(picked, (count, 128))

    for load in loads[1:4]:
        load.wait()
    rows_ref[0] = column_of(conv_ref[...])
    rows_ref[1] = column_of(speed_ref[...])
    for part in range(8):
        pt_part = plane_ref[0, :, 128 * part : 128 * part + 128]
        for y in range(16):
            pt[y, part : part + 1, :] = pt_part[y : y + 1, :]

    row_copy = out_copy(rows_ref, row_vals.at[core], row_send, row_recv, partner)
    row_copy.start()
    row_vals[core] = rows_ref[...]

    @pl.loop(0, 8)
    def _(i):
        spread_start("plane", (i + me_s + 1) % 8)

    for load in loads[4:]:
        load.wait()
    kernel_row = jnp.dot(
        jnp.broadcast_to(filter_ref[...], (8, 512)), table_ref[...],
        precision=lax.Precision.HIGHEST, preferred_element_type=jnp.float32,
    )[0:1]
    rolled = pltpu.roll(jnp.broadcast_to(kernel_row, (256, 1024)), 0, 1, stride=1, stride_axis=0)
    b0, b1, b2, b3 = (rolled[:, 256 * i : 256 * i + 256] for i in range(4))
    for i, block in enumerate(
        (
            0.25 * ((b0 + b2) + (b1 + b3)),
            0.25 * ((b0 + b2) - (b1 + b3)),
            0.5 * (b0 - b2),
            0.5 * (b1 - b3),
        )
    ):
        weights[0, i], weights[1, i] = halves(block)
    op_parts = halves(op_ref[...])
    source_index = lax.broadcasted_iota(jnp.int32, (64, 192), 0)
    column = lax.broadcasted_iota(jnp.int32, (64, 192), 1)
    into_high = ((column % 64 == source_index) & (column < 128)).astype(jnp.bfloat16)
    into_low = ((column % 64 == source_index) & (column >= 128)).astype(jnp.bfloat16)
    op_cat[...] = (mul(op_parts[0], into_high) + mul(op_parts[1], into_low)).astype(jnp.bfloat16)
    col_ref[...] = column_of(inlet_ref[...])

    @pl.loop(0, 8)
    def _(i):
        c = arrival(i)
        spread_arrived("vel", c)

        @pl.when(low_sends(0, c))
        def _():
            low_copy(0, c).start()

        @pl.when(high_sends(0, c))
        def _():
            high_copy(0, c).start()

        j = (i + first_eddy) % 8
        for y in range(PAIR):
            et[PAIR * j + y] = jnp.squeeze(eddy_ref[:, pl.ds(PAIR * j + y, 1), :], axis=1)
        spread_start("eddy", j)

    @pl.when(relays_in)
    def _():
        @pl.loop(0, 4)
        def _(k):
            arrived, onward = forward_eddy(k)
            arrived.wait()
            onward.start()

    def products(n):
        for y in range(PAIR):
            up, down = halves(state[n, y])
            dx[y] = mul(op_cat[...], jnp.concatenate([up, down, up], axis=0))
        u = state[n].reshape(128, 1024)
        v0, v1, v2, v3 = (u[:, 256 * i : 256 * i + 256] for i in range(4))
        even, odd = v0 + v2, v1 + v3

        def times(value, *which):
            up, down = halves(value)
            count = value.shape[0]
            both = jnp.concatenate([up, down], axis=0)
            found = []
            for i in which:
                wide = mul(both, weights[0, i])
                found.append(wide[:count] + wide[count:] + mul(up, weights[1, i]))
            return found

        (first,) = times(even + odd, 0)
        (second,) = times(even - odd, 1)
        straight, crossed = times(jnp.concatenate([v0 - v2, v1 - v3], axis=0), 2, 3)
        diff0 = straight[:128] - crossed[128:]
        diff1 = crossed[:128] + straight[128:]
        for i, part in enumerate(
            (
                (first + second) + diff0,
                (first - second) + diff1,
                (first + second) - diff0,
                (first - second) - diff1,
            )
        ):
            sz[:, :, 256 * i : 256 * i + 256] = part.reshape(PAIR, 64, 256)

    source_core = home % 2

    def row_value(which, y):
        row = PAIR * offset + y
        value = row_vals[source_core, which, pl.ds(row, 1), :]
        return jnp.concatenate([jnp.broadcast_to(value, (8, 128))] * 8, axis=1)

    def combine(n):
        if n == 0:
            row_copy.wait_recv()

            @pl.loop(0, 8)
            def _(s):
                spread_arrived("plane", s)

        step = (0.5 * time_step, 0.5 * time_step, time_step, 0.0)[n]
        share = time_step / 6.0 * (1.0, 2.0, 2.0, 1.0)[n]
        gusts = []
        for y in range(PAIR):
            tile = inlets[record_ref[n], y]
            gusts.append(
                jnp.concatenate(
                    [jnp.broadcast_to(tile[i : i + 1], (8, 128)) for i in range(8)], axis=1
                )
            )
        conv = [row_value(0, y) for y in range(PAIR)]
        speed = [row_value(1, y) for y in range(PAIR)]

        @pl.loop(0, 8)
        def _(i):
            c = arrival(i) if n == 0 else i
            if n == 0:
                spread_arrived("eddy", c)
            low_copy(n, c).wait_recv()
            high_copy(n, c).wait_recv()
            r = rows8(c)
            column = jnp.concatenate([col_ref[r, :]] * 8, axis=1)
            rows = [low[n, 0, r], low[n, 1, r], state[n, 0, r], state[n, 1, r], high[n, 0, r], high[n, 1, r]]
            for y in range(PAIR):
                u = rows[y + 2]
                second = (
                    16.0 * (rows[y + 1] + rows[y + 3]) - (rows[y] + rows[y + 4]) - 30.0 * u
                ) * (1.0 / 12.0)
                rate = (
                    eddy[y, r] * second
                    - (conv[y] + u) * (dx[y, r] + column * gusts[y])
                    - speed[y] * sz[y, r]
                )
                if n == 0:
                    total[y, r] = u + share * rate
                    state[1, y, r] = u + step * rate
                elif n < 3:
                    total[y, r] += share * rate
                    state[n + 1, y, r] = state[0, y, r] + step * rate
                else:
                    state[4, y, r] = total[y, r] + share * rate
            if n < 3:
                low_copy(n + 1, c).start()
                high_copy(n + 1, c).start()
            else:
                remote, local = result_copy(c)
                mine = (c == me_s) & (home == me_p)

                @pl.when(jnp.logical_not(mine))
                def _():
                    remote.start()

                @pl.when(mine)
                def _():
                    local().start()

    for n in range(4):
        products(n)
        combine(n)

    @pl.when(relays_in)
    def _():
        for k in range(4):
            forward_eddy(k)[1].wait_send()

    @pl.when(crossing)
    def _():
        edge_copy(True).wait_send()

    spread_sent("vel")
    spread_sent("plane")
    spread_sent("eddy")
    row_copy.wait_send()

    @pl.loop(0, 8)
    def _(c):
        for n in range(4):

            @pl.when(low_sends(n, c))
            def _():
                low_copy(n, c).wait_send()

            @pl.when(high_sends(n, c))
            def _():
                high_copy(n, c).wait_send()

        mine = (c == me_s) & (home == me_p)

        @pl.when(jnp.logical_not(mine))
        def _():
            result_copy(c)[0].wait_send()

        pltpu.make_async_copy(
            state.at[4, :, rows8(0)], out_ref.at[pl.ds(PAIR * c, PAIR)], out_recv.at[c]
        ).wait()


def ring_shards(
    velocity, eddy_visc, stream_op, inlet_col, planes, record, convection, span_speed, span_filter
):
    span_len = velocity.shape[2]
    half = span_len // 2
    modes = np.arange(half)[:, None]
    angle = (modes * np.arange(span_len)[None, :] % span_len) * (2.0 * np.pi / span_len)
    table = (-2.0 / span_len * modes / half * np.sin(angle)).astype(np.float32)
    f32, dma = jnp.float32, pltpu.SemaphoreType.DMA
    result = pl.pallas_call(
        ring_kernel,
        out_shape=pltpu.VMEM((16, 8, 1024), f32),
        in_specs=[pl.BlockSpec(memory_space=pltpu.HBM)] * 10,
        out_specs=pl.BlockSpec(memory_space=pltpu.VMEM),
        scratch_shapes=[
            pltpu.VMEM((8, 16, 1024), f32),
            pltpu.VMEM((8, 16, 1024), f32),
            pltpu.VMEM((64, 64), f32),
            pltpu.VMEM((1, 64), f32),
            pltpu.VMEM((1, 16, 1024), f32),
            pltpu.SMEM((4,), jnp.int32),
            pltpu.VMEM((1, 16), f32),
            pltpu.VMEM((1, 16), f32),
            pltpu.VMEM((1, 512), f32),
            pltpu.VMEM((512, 1024), f32),
            dma((10,)),
            pltpu.VMEM((64, 128), f32),
            pltpu.VMEM((2, 16, 128), f32),
            pltpu.VMEM((16, 8, 1024), f32),
            pltpu.VMEM((16, 8, 1024), f32),
            pltpu.VMEM((16, 8, 128), f32),
            pltpu.VMEM((5, 2, 64, 1024), f32),
            pltpu.VMEM((2, 64, 1024), f32),
            pltpu.VMEM((8, 2, 8, 128), f32),
            pltpu.VMEM((2, 2, 16, 128), f32),
            pltpu.VMEM((4, 2, 64, 1024), f32),
            pltpu.VMEM((4, 2, 64, 1024), f32),
            pltpu.VMEM((2, 64, 1024), f32),
            pltpu.VMEM((2, 64, 1024), f32),
            pltpu.VMEM((2, 64, 1024), f32),
            pltpu.VMEM((2, 4, 256, 256), jnp.bfloat16),
            pltpu.VMEM((64, 192), jnp.bfloat16),
            dma((8,)), dma((8,)), dma((8,)), dma((8,)), dma((8,)), dma((8,)), dma, dma,
            dma((4, 8)), dma((4, 8)), dma((4, 8)), dma((4, 8)), dma((8,)), dma((8,)),
            pltpu.VMEM((4, 2, 8, 1024), f32), dma((4,)), dma((4,)), dma,
        ],
        compiler_params=pltpu.CompilerParams(
            collective_id=0, has_side_effects=True, vmem_limit_bytes=56 * 2**20
        ),
    )(
        velocity,
        eddy_visc,
        stream_op,
        inlet_col[None, :],
        planes,
        record,
        convection[None, :],
        span_speed[None, :],
        span_filter[None, :],
        jnp.asarray(table),
    )
    return result.transpose(1, 0, 2)


def either(velocity, *others):
    fits = (
        lax.axis_size("stream") == 8
        and lax.axis_size("pitch") == 4
        and velocity.shape == (8, 16, 1024)
    )
    return (ring_shards if fits else shards)(velocity, *others)


def solution(mesh):
    placed = (
        P("stream", "pitch", None),
        P("stream", "pitch", None),
        P(),
        P(),
        P("stream", "pitch", None),
        P(),
        P("pitch"),
        P("pitch"),
        P(),
    )
    return jax.shard_map(
        either, mesh=mesh, in_specs=placed, out_specs=P("stream", "pitch", None), check_vma=False
    )
```

```python
import math

import jax
import jax.numpy as jnp
import numpy as np
from jax import lax
from jax.experimental import pallas as pl
from jax.experimental.pallas import tpu as pltpu
from jax.sharding import PartitionSpec as P

time_step = 0.25


def spread(shard, axis, root):
    mine = lax.axis_index(axis) == root
    return lax.psum(jnp.where(mine, shard, jnp.zeros_like(shard)), axis)


def with_halo(shard, sides, width):
    for axis, dim in sides:
        peers, length = (lax.axis_size(axis), shard.shape[dim])
        up = [(i, (i + 1) % peers) for i in range(peers)]
        down = [(j, i) for i, j in up]
        last = lax.slice_in_dim(shard, length - width, length, axis=dim)
        initial = lax.slice_in_dim(shard, 0, width, axis=dim)
        before = lax.ppermute(last, axis, up)
        after = lax.ppermute(initial, axis, down)
        shard = jnp.concatenate([before, shard, after], axis=dim)
    return shard


def pitch_second(padded):
    return (
        -padded[:, 0:-4]
        + 16.0 * padded[:, 1:-3]
        - 30.0 * padded[:, 2:-2]
        + 16.0 * padded[:, 3:-1]
        - padded[:, 4:]
    ) / 12.0


def shards(
    velocity, eddy_visc, stream_op, inlet_col, planes, record, convection, span_speed, span_filter
):
    cells_x, cells_y, span_len = velocity.shape
    stream_len = stream_op.shape[0]
    span_piece = span_len // lax.axis_size("stream")
    position = lax.axis_index("stream")
    half = span_len // 2
    rows_index = lax.iota(jnp.int32, span_len)[:, None]
    mode_index = lax.iota(jnp.int32, half)[None, :]
    angle = (rows_index * mode_index % span_len).astype(jnp.float32) * (2.0 * math.pi / span_len)
    table_dft = jnp.concatenate([jnp.cos(angle), jnp.sin(angle)], axis=1)
    gains = span_filter * lax.iota(jnp.float32, half) / half
    conv_rows = convection[None, :, None]
    span_rows = span_speed[None, :, None]

    def inlet_at(section):
        whole = spread(planes[0], "stream", record[section])
        return lax.dynamic_slice_in_dim(whole, position * span_piece, span_piece, 1)

    def span_part(state):
        flat = state.reshape(-1, span_len)
        coeffs = jnp.dot(
            flat, table_dft, precision=lax.Precision.HIGHEST, preferred_element_type=jnp.float32
        )
        mixed = jnp.concatenate([coeffs[:, half:] * gains, -coeffs[:, :half] * gains], axis=1)
        back = lax.dot_general(
            mixed,
            table_dft,
            (((1,), (1,)), ((), ())),
            precision=lax.Precision.HIGHEST,
            preferred_element_type=jnp.float32,
        )
        return (back * (2.0 / span_len)).reshape(state.shape)

    def section_rate(state, section):
        inlet_slice = inlet_at(section)
        pencil = lax.all_to_all(state, "stream", split_axis=2, concat_axis=0, tiled=True)
        stream_deriv = jnp.dot(
            stream_op,
            pencil.reshape(stream_len, -1),
            precision=lax.Precision.HIGHEST,
            preferred_element_type=jnp.float32,
        )
        stream_deriv = (
            stream_deriv.reshape(pencil.shape) + inlet_col[:, None, None] * inlet_slice[None, :, :]
        )
        returned = lax.all_to_all(stream_deriv, "stream", split_axis=0, concat_axis=2, tiled=True)
        padded = with_halo(state, (("pitch", 1),), 2)
        local_terms = -(conv_rows + state) * returned + eddy_visc * pitch_second(padded)
        return local_terms - span_rows * span_part(state)

    first = section_rate(velocity, 0)
    second = section_rate(velocity + 0.5 * time_step * first, 1)
    third = section_rate(velocity + 0.5 * time_step * second, 2)
    fourth = section_rate(velocity + time_step * third, 3)
    return velocity + time_step / 6.0 * (first + 2.0 * second + 2.0 * third + fourth)


CHUNK = 8
PAIR = 2
MESH_ID = pl.DeviceIdType.MESH


def place_of(rank):
    spot, turn = rank // 2, rank % 2
    plane, step = spot // 8, spot % 8
    along = step + plane * (7 - 2 * step)
    depth = along // 2
    core = (plane + depth // 2 + step + turn) % 2
    return 2 * depth + (along + 1) // 2 % 2, 2 * plane + core


def rank_of(stream, pitch):
    depth, side, plane, core = stream // 2, stream % 2, pitch // 2, pitch % 2
    along = 2 * depth + (side + depth) % 2
    step = along + plane * (7 - 2 * along)
    return 2 * (8 * plane + step) + (core + plane + depth // 2 + step) % 2


def halves(value):
    high = value.astype(jnp.bfloat16)
    return high, (value - high.astype(jnp.float32)).astype(jnp.bfloat16)


def mul(left, right):
    return jnp.dot(left, right, preferred_element_type=jnp.float32)


def ring_kernel(
    vel_hbm, eddy_hbm, op_hbm, col_hbm, plane_hbm, record_hbm, conv_hbm, speed_hbm, filter_hbm, table_hbm,
    out_ref,
    vel_ref, eddy_ref, op_ref, inlet_ref, plane_ref, record_ref, conv_ref, speed_ref, filter_ref, table_ref,
    in_sems, col_ref, rows_ref,
    vt, et, pt, state, eddy, inlets, row_vals, low, high, total, dx, sz, weights, op_cat,
    vel_send, vel_recv, eddy_send, eddy_recv, pl_send, pl_recv, row_send, row_recv,
    low_send, low_recv, high_send, high_recv, out_send, out_recv,
    eddy_via, eddy_via_recv, eddy_on, edge_send, landed,
):
    me_s, me_p = lax.axis_index("stream"), lax.axis_index("pitch")
    me = rank_of(me_s, me_p)
    home = me // 8
    offset = me % 8
    above = place_of((me + 1) % 32)
    below = place_of((me + 31) % 32)
    partner = (me_s, me_p + 1 - 2 * (me_p % 2))
    core = me_p % 2
    upper = me_s // 4
    group_upper = (me_p + 1) // 2 % 2
    feeds = (me_s == 2) | (me_s == 4)
    relays = (me_s == 3) | (me_s == 5)
    feeds_in = feeds & (group_upper != upper)
    relays_in = relays & (group_upper == upper)
    crossing = group_upper != upper
    mirrored = (me_s + 2 * (1 - upper)) % 4
    first_vel = jnp.where(crossing & (mirrored < 2), 6, 2)
    first_eddy = jnp.where(crossing & (mirrored == 1), 6, 2)
    edge = 7 * (1 - core)
    edge_peer = place_of((8 * me_p + edge + 33 - 2 * core) % 32)
    ends_low, ends_high = me % 16 == 7, me % 16 == 8
    inner = (offset >= 2) & (offset <= 5)

    def arrival(i):
        turn = jnp.where(inner, 7 - i % 4, 4 + i % 4)
        return jnp.where(i < 4, 4 * upper + i % 4, jnp.where(upper == 1, (turn + 2) % 4, turn))

    loads = [
        pltpu.make_async_copy(source, target, in_sems.at[i])
        for i, (source, target) in enumerate(
            (
                (vel_hbm, vel_ref), (plane_hbm, plane_ref), (conv_hbm, conv_ref), (speed_hbm, speed_ref),
                (eddy_hbm, eddy_ref), (filter_hbm, filter_ref), (table_hbm, table_ref), (op_hbm, op_ref),
                (col_hbm, inlet_ref), (record_hbm, record_ref),
            )
        )
    ]
    for load in loads[:4]:
        load.start()

    barrier = pltpu.get_barrier_semaphore()

    @pl.loop(1, 32)
    def _(step):
        other = (me_s * 4 + me_p + step) % 32
        pl.semaphore_signal(barrier, inc=1, device_id=(other // 4, other % 4), device_id_type=MESH_ID)

    def rows8(index):
        return pl.ds(pl.multiple_of(index * CHUNK, CHUNK), CHUNK)

    def out_copy(src, dst, send, recv, device):
        return pltpu.make_async_remote_copy(
            src_ref=src, dst_ref=dst, send_sem=send, recv_sem=recv, device_id=device,
            device_id_type=MESH_ID,
        )

    def spread_copy(kind, j):
        src, dst, send, recv = {
            "vel": (vt, state.at[0], vel_send, vel_recv),
            "eddy": (et, eddy, eddy_send, eddy_recv),
            "plane": (pt, inlets, pl_send, pl_recv),
        }[kind]
        source = src.at[pl.ds(PAIR * j, PAIR)]
        target = dst.at[me_s] if kind == "plane" else dst.at[:, rows8(me_s)]
        rank = 8 * me_p + j
        return (
            rank,
            out_copy(source, target, send.at[j], recv.at[me_s], place_of(rank)),
            lambda: pltpu.make_async_copy(source, target, recv.at[me_s]),
        )

    def spread_start(kind, j):
        rank, remote, local = spread_copy(kind, j)

        via = feeds_in & (j >= 2) & (j <= 5) if kind == "eddy" else False

        @pl.when((rank != me) & jnp.logical_not(via))
        def _():
            remote.start()

        @pl.when(rank == me)
        def _():
            local().start()

        if kind == "eddy":

            @pl.when(via)
            def _():
                k = (j + 6) % 8
                out_copy(
                    et.at[pl.ds(PAIR * j, PAIR)], eddy_via.at[k], eddy_send.at[j], eddy_via_recv.at[k],
                    (me_s + 1, me_p + 1 - 2 * core),
                ).start()

    def forward_eddy(k):
        source = (me_s + 7) % 8
        return (
            pltpu.make_async_copy(eddy_via.at[k], eddy_via.at[k], eddy_via_recv.at[k]),
            out_copy(
                eddy_via.at[k], eddy.at[:, rows8(source)], eddy_on.at[k], eddy_recv.at[source],
                place_of(8 * (me_p + 1 - 2 * core) + 2 + k),
            ),
        )

    def edge_copy(to_low):
        dst, recv = (low, low_recv) if to_low else (high, high_recv)
        return out_copy(
            vt.at[pl.ds(PAIR * edge, PAIR)], dst.at[0, :, rows8(me_s)], edge_send, recv.at[0, me_s],
            edge_peer,
        )

    def edge_start(j):
        @pl.when(crossing & (j == edge) & (core == 0))
        def _():
            edge_copy(True).start()

        @pl.when(crossing & (j == edge) & (core == 1))
        def _():
            edge_copy(False).start()

    def low_sends(n, c):
        return jnp.logical_not(ends_low & (c // 4 != upper)) if n == 0 else True

    def high_sends(n, c):
        return jnp.logical_not(ends_high & (c // 4 != upper)) if n == 0 else True

    def spread_sent(kind):
        @pl.loop(0, 8)
        def _(j):
            rank, remote, _local = spread_copy(kind, j)

            @pl.when(rank != me)
            def _():
                remote.wait_send()

    def spread_arrived(kind, s):
        src, dst, send, recv = {
            "vel": (vt, state.at[0], vel_send, vel_recv),
            "eddy": (et, eddy, eddy_send, eddy_recv),
            "plane": (pt, inlets, pl_send, pl_recv),
        }[kind]
        target = dst.at[s] if kind == "plane" else dst.at[:, rows8(s)]
        pltpu.make_async_copy(src.at[pl.ds(0, PAIR)], target, recv.at[s]).wait()

    def low_copy(n, c):
        return out_copy(
            state.at[n, :, rows8(c)], low.at[n, :, rows8(c)], low_send.at[n, c], low_recv.at[n, c], above
        )

    def high_copy(n, c):
        return out_copy(
            state.at[n, :, rows8(c)], high.at[n, :, rows8(c)], high_send.at[n, c], high_recv.at[n, c],
            below,
        )

    def result_copy(s):
        source = state.at[4, :, rows8(s)]
        target = landed.at[pl.ds(PAIR * offset, PAIR)]
        return (
            out_copy(source, target, out_send.at[s], out_recv.at[offset], (s, home)),
            lambda: pltpu.make_async_copy(source, target, out_recv.at[offset]),
        )

    loads[0].wait()
    for load in loads[4:]:
        load.start()

    pl.semaphore_wait(barrier, 31)

    @pl.loop(0, 8)
    def _(i):
        j = (i + first_vel) % 8
        for y in range(PAIR):
            vt[PAIR * j + y] = jnp.squeeze(vel_ref[:, pl.ds(PAIR * j + y, 1), :], axis=1)
        spread_start("vel", j)
        edge_start(j)

    def column_of(row):
        count = row.shape[1]
        own = lax.broadcasted_iota(jnp.int32, (count, count), 0) == lax.broadcasted_iota(
            jnp.int32, (count, count), 1
        )
        picked = jnp.sum(jnp.where(own, jnp.broadcast_to(row, (count, count)), 0.0), axis=1, keepdims=True)
        return jnp.broadcast_to(picked, (count, 128))

    for load in loads[1:4]:
        load.wait()
    rows_ref[0] = column_of(conv_ref[...])
    rows_ref[1] = column_of(speed_ref[...])
    for part in range(8):
        pt_part = plane_ref[0, :, 128 * part : 128 * part + 128]
        for y in range(16):
            pt[y, part : part + 1, :] = pt_part[y : y + 1, :]

    row_copy = out_copy(rows_ref, row_vals.at[core], row_send, row_recv, partner)
    row_copy.start()
    row_vals[core] = rows_ref[...]

    @pl.loop(0, 8)
    def _(i):
        spread_start("plane", (i + me_s + 1) % 8)

    for load in loads[4:]:
        load.wait()
    kernel_row = jnp.dot(
        jnp.broadcast_to(filter_ref[...], (8, 512)), table_ref[...],
        precision=lax.Precision.HIGHEST, preferred_element_type=jnp.float32,
    )[0:1]
    rolled = pltpu.roll(jnp.broadcast_to(kernel_row, (256, 1024)), 0, 1, stride=1, stride_axis=0)
    b0, b1, b2, b3 = (rolled[:, 256 * i : 256 * i + 256] for i in range(4))
    for i, block in enumerate(
        (
            0.25 * ((b0 + b2) + (b1 + b3)),
            0.25 * ((b0 + b2) - (b1 + b3)),
            0.5 * (b0 - b2),
            0.5 * (b1 - b3),
        )
    ):
        weights[0, i], weights[1, i] = halves(block)
    op_parts = halves(op_ref[...])
    source_index = lax.broadcasted_iota(jnp.int32, (64, 192), 0)
    column = lax.broadcasted_iota(jnp.int32, (64, 192), 1)
    into_high = ((column % 64 == source_index) & (column < 128)).astype(jnp.bfloat16)
    into_low = ((column % 64 == source_index) & (column >= 128)).astype(jnp.bfloat16)
    op_cat[...] = (mul(op_parts[0], into_high) + mul(op_parts[1], into_low)).astype(jnp.bfloat16)
    col_ref[...] = column_of(inlet_ref[...])

    @pl.loop(0, 8)
    def _(i):
        c = arrival(i)
        spread_arrived("vel", c)

        @pl.when(low_sends(0, c))
        def _():
            low_copy(0, c).start()

        @pl.when(high_sends(0, c))
        def _():
            high_copy(0, c).start()

        j = (i + first_eddy) % 8
        for y in range(PAIR):
            et[PAIR * j + y] = jnp.squeeze(eddy_ref[:, pl.ds(PAIR * j + y, 1), :], axis=1)
        spread_start("eddy", j)

    @pl.when(relays_in)
    def _():
        @pl.loop(0, 4)
        def _(k):
            arrived, onward = forward_eddy(k)
            arrived.wait()
            onward.start()

    def products(n):
        for y in range(PAIR):
            up, down = halves(state[n, y])
            dx[y] = mul(op_cat[...], jnp.concatenate([up, down, up], axis=0))
        u = state[n].reshape(128, 1024)
        v0, v1, v2, v3 = (u[:, 256 * i : 256 * i + 256] for i in range(4))
        even, odd = v0 + v2, v1 + v3

        def times(value, *which):
            up, down = halves(value)
            count = value.shape[0]
            both = jnp.concatenate([up, down], axis=0)
            found = []
            for i in which:
                wide = mul(both, weights[0, i])
                found.append(wide[:count] + wide[count:] + mul(up, weights[1, i]))
            return found

        (first,) = times(even + odd, 0)
        (second,) = times(even - odd, 1)
        straight, crossed = times(jnp.concatenate([v0 - v2, v1 - v3], axis=0), 2, 3)
        diff0 = straight[:128] - crossed[128:]
        diff1 = crossed[:128] + straight[128:]
        for i, part in enumerate(
            (
                (first + second) + diff0,
                (first - second) + diff1,
                (first + second) - diff0,
                (first - second) - diff1,
            )
        ):
            sz[:, :, 256 * i : 256 * i + 256] = part.reshape(PAIR, 64, 256)

    source_core = home % 2

    def row_value(which, y):
        row = PAIR * offset + y
        value = row_vals[source_core, which, pl.ds(row, 1), :]
        return jnp.concatenate([jnp.broadcast_to(value, (8, 128))] * 8, axis=1)

    def combine(n):
        if n == 0:
            row_copy.wait_recv()

            @pl.loop(0, 8)
            def _(s):
                spread_arrived("plane", s)

        step = (0.5 * time_step, 0.5 * time_step, time_step, 0.0)[n]
        share = time_step / 6.0 * (1.0, 2.0, 2.0, 1.0)[n]
        gusts = []
        for y in range(PAIR):
            tile = inlets[record_ref[n], y]
            gusts.append(
                jnp.concatenate(
                    [jnp.broadcast_to(tile[i : i + 1], (8, 128)) for i in range(8)], axis=1
                )
            )
        conv = [row_value(0, y) for y in range(PAIR)]
        speed = [row_value(1, y) for y in range(PAIR)]

        @pl.loop(0, 8)
        def _(i):
            c = arrival(i) if n == 0 else i
            if n == 0:
                spread_arrived("eddy", c)
            low_copy(n, c).wait_recv()
            high_copy(n, c).wait_recv()
            r = rows8(c)
            column = jnp.concatenate([col_ref[r, :]] * 8, axis=1)
            rows = [low[n, 0, r], low[n, 1, r], state[n, 0, r], state[n, 1, r], high[n, 0, r], high[n, 1, r]]
            for y in range(PAIR):
                u = rows[y + 2]
                second = (
                    16.0 * (rows[y + 1] + rows[y + 3]) - (rows[y] + rows[y + 4]) - 30.0 * u
                ) * (1.0 / 12.0)
                rate = (
                    eddy[y, r] * second
                    - (conv[y] + u) * (dx[y, r] + column * gusts[y])
                    - speed[y] * sz[y, r]
                )
                if n == 0:
                    total[y, r] = u + share * rate
                    state[1, y, r] = u + step * rate
                elif n < 3:
                    total[y, r] += share * rate
                    state[n + 1, y, r] = state[0, y, r] + step * rate
                else:
                    state[4, y, r] = total[y, r] + share * rate
            if n < 3:
                low_copy(n + 1, c).start()
                high_copy(n + 1, c).start()
            else:
                remote, local = result_copy(c)
                mine = (c == me_s) & (home == me_p)

                @pl.when(jnp.logical_not(mine))
                def _():
                    remote.start()

                @pl.when(mine)
                def _():
                    local().start()

    for n in range(4):
        products(n)
        combine(n)

    @pl.when(relays_in)
    def _():
        for k in range(4):
            forward_eddy(k)[1].wait_send()

    @pl.when(crossing)
    def _():
        edge_copy(True).wait_send()

    spread_sent("vel")
    spread_sent("plane")
    spread_sent("eddy")
    row_copy.wait_send()

    @pl.loop(0, 8)
    def _(c):
        for n in range(4):

            @pl.when(low_sends(n, c))
            def _():
                low_copy(n, c).wait_send()

            @pl.when(high_sends(n, c))
            def _():
                high_copy(n, c).wait_send()

        mine = (c == me_s) & (home == me_p)

        @pl.when(jnp.logical_not(mine))
        def _():
            result_copy(c)[0].wait_send()

        pltpu.make_async_copy(
            state.at[4, :, rows8(0)], landed.at[pl.ds(PAIR * c, PAIR)], out_recv.at[c]
        ).wait()
        for y in range(PAIR):
            out_ref[:, pl.ds(PAIR * c + y, 1), :] = jnp.expand_dims(landed[PAIR * c + y], 1)


def ring_shards(
    velocity, eddy_visc, stream_op, inlet_col, planes, record, convection, span_speed, span_filter
):
    span_len = velocity.shape[2]
    half = span_len // 2
    modes = np.arange(half)[:, None]
    angle = (modes * np.arange(span_len)[None, :] % span_len) * (2.0 * np.pi / span_len)
    table = (-2.0 / span_len * modes / half * np.sin(angle)).astype(np.float32)
    f32, dma = jnp.float32, pltpu.SemaphoreType.DMA
    result = pl.pallas_call(
        ring_kernel,
        out_shape=pltpu.VMEM((8, 16, 1024), f32),
        in_specs=[pl.BlockSpec(memory_space=pltpu.HBM)] * 10,
        out_specs=pl.BlockSpec(memory_space=pltpu.VMEM),
        scratch_shapes=[
            pltpu.VMEM((8, 16, 1024), f32),
            pltpu.VMEM((8, 16, 1024), f32),
            pltpu.VMEM((64, 64), f32),
            pltpu.VMEM((1, 64), f32),
            pltpu.VMEM((1, 16, 1024), f32),
            pltpu.SMEM((4,), jnp.int32),
            pltpu.VMEM((1, 16), f32),
            pltpu.VMEM((1, 16), f32),
            pltpu.VMEM((1, 512), f32),
            pltpu.VMEM((512, 1024), f32),
            dma((10,)),
            pltpu.VMEM((64, 128), f32),
            pltpu.VMEM((2, 16, 128), f32),
            pltpu.VMEM((16, 8, 1024), f32),
            pltpu.VMEM((16, 8, 1024), f32),
            pltpu.VMEM((16, 8, 128), f32),
            pltpu.VMEM((5, 2, 64, 1024), f32),
            pltpu.VMEM((2, 64, 1024), f32),
            pltpu.VMEM((8, 2, 8, 128), f32),
            pltpu.VMEM((2, 2, 16, 128), f32),
            pltpu.VMEM((4, 2, 64, 1024), f32),
            pltpu.VMEM((4, 2, 64, 1024), f32),
            pltpu.VMEM((2, 64, 1024), f32),
            pltpu.VMEM((2, 64, 1024), f32),
            pltpu.VMEM((2, 64, 1024), f32),
            pltpu.VMEM((2, 4, 256, 256), jnp.bfloat16),
            pltpu.VMEM((64, 192), jnp.bfloat16),
            dma((8,)), dma((8,)), dma((8,)), dma((8,)), dma((8,)), dma((8,)), dma, dma,
            dma((4, 8)), dma((4, 8)), dma((4, 8)), dma((4, 8)), dma((8,)), dma((8,)),
            pltpu.VMEM((4, 2, 8, 1024), f32), dma((4,)), dma((4,)), dma,
            pltpu.VMEM((16, 8, 1024), f32),
        ],
        compiler_params=pltpu.CompilerParams(
            collective_id=0, has_side_effects=True, vmem_limit_bytes=56 * 2**20
        ),
    )(
        velocity,
        eddy_visc,
        stream_op,
        inlet_col[None, :],
        planes,
        record,
        convection[None, :],
        span_speed[None, :],
        span_filter[None, :],
        jnp.asarray(table),
    )
    return result


def either(velocity, *others):
    fits = (
        lax.axis_size("stream") == 8
        and lax.axis_size("pitch") == 4
        and velocity.shape == (8, 16, 1024)
    )
    return (ring_shards if fits else shards)(velocity, *others)


def solution(mesh):
    placed = (
        P("stream", "pitch", None),
        P("stream", "pitch", None),
        P(),
        P(),
        P("stream", "pitch", None),
        P(),
        P("pitch"),
        P("pitch"),
        P(),
    )
    return jax.shard_map(
        either, mesh=mesh, in_specs=placed, out_specs=P("stream", "pitch", None), check_vma=False
    )
```

```python
import math

import jax
import jax.numpy as jnp
import numpy as np
from jax import lax
from jax.experimental import pallas as pl
from jax.experimental.pallas import tpu as pltpu
from jax.sharding import PartitionSpec as P

time_step = 0.25


def spread(shard, axis, root):
    mine = lax.axis_index(axis) == root
    return lax.psum(jnp.where(mine, shard, jnp.zeros_like(shard)), axis)


def with_halo(shard, sides, width):
    for axis, dim in sides:
        peers, length = (lax.axis_size(axis), shard.shape[dim])
        up = [(i, (i + 1) % peers) for i in range(peers)]
        down = [(j, i) for i, j in up]
        last = lax.slice_in_dim(shard, length - width, length, axis=dim)
        initial = lax.slice_in_dim(shard, 0, width, axis=dim)
        before = lax.ppermute(last, axis, up)
        after = lax.ppermute(initial, axis, down)
        shard = jnp.concatenate([before, shard, after], axis=dim)
    return shard


def pitch_second(padded):
    return (
        -padded[:, 0:-4]
        + 16.0 * padded[:, 1:-3]
        - 30.0 * padded[:, 2:-2]
        + 16.0 * padded[:, 3:-1]
        - padded[:, 4:]
    ) / 12.0


def shards(
    velocity, eddy_visc, stream_op, inlet_col, planes, record, convection, span_speed, span_filter
):
    cells_x, cells_y, span_len = velocity.shape
    stream_len = stream_op.shape[0]
    span_piece = span_len // lax.axis_size("stream")
    position = lax.axis_index("stream")
    half = span_len // 2
    rows_index = lax.iota(jnp.int32, span_len)[:, None]
    mode_index = lax.iota(jnp.int32, half)[None, :]
    angle = (rows_index * mode_index % span_len).astype(jnp.float32) * (2.0 * math.pi / span_len)
    table_dft = jnp.concatenate([jnp.cos(angle), jnp.sin(angle)], axis=1)
    gains = span_filter * lax.iota(jnp.float32, half) / half
    conv_rows = convection[None, :, None]
    span_rows = span_speed[None, :, None]

    def inlet_at(section):
        whole = spread(planes[0], "stream", record[section])
        return lax.dynamic_slice_in_dim(whole, position * span_piece, span_piece, 1)

    def span_part(state):
        flat = state.reshape(-1, span_len)
        coeffs = jnp.dot(
            flat, table_dft, precision=lax.Precision.HIGHEST, preferred_element_type=jnp.float32
        )
        mixed = jnp.concatenate([coeffs[:, half:] * gains, -coeffs[:, :half] * gains], axis=1)
        back = lax.dot_general(
            mixed,
            table_dft,
            (((1,), (1,)), ((), ())),
            precision=lax.Precision.HIGHEST,
            preferred_element_type=jnp.float32,
        )
        return (back * (2.0 / span_len)).reshape(state.shape)

    def section_rate(state, section):
        inlet_slice = inlet_at(section)
        pencil = lax.all_to_all(state, "stream", split_axis=2, concat_axis=0, tiled=True)
        stream_deriv = jnp.dot(
            stream_op,
            pencil.reshape(stream_len, -1),
            precision=lax.Precision.HIGHEST,
            preferred_element_type=jnp.float32,
        )
        stream_deriv = (
            stream_deriv.reshape(pencil.shape) + inlet_col[:, None, None] * inlet_slice[None, :, :]
        )
        returned = lax.all_to_all(stream_deriv, "stream", split_axis=0, concat_axis=2, tiled=True)
        padded = with_halo(state, (("pitch", 1),), 2)
        local_terms = -(conv_rows + state) * returned + eddy_visc * pitch_second(padded)
        return local_terms - span_rows * span_part(state)

    first = section_rate(velocity, 0)
    second = section_rate(velocity + 0.5 * time_step * first, 1)
    third = section_rate(velocity + 0.5 * time_step * second, 2)
    fourth = section_rate(velocity + time_step * third, 3)
    return velocity + time_step / 6.0 * (first + 2.0 * second + 2.0 * third + fourth)


CHUNK = 8
PAIR = 2
MESH_ID = pl.DeviceIdType.MESH


def place_of(rank):
    spot, turn = rank // 2, rank % 2
    plane, step = spot // 8, spot % 8
    along = step + (1 - plane) * (7 - 2 * step)
    depth = along // 2
    core = (plane + depth // 2 + step + turn + 1) % 2
    return 2 * depth + (along + 1) // 2 % 2, 2 * plane + core


def rank_of(stream, pitch):
    depth, side, plane, core = stream // 2, stream % 2, pitch // 2, pitch % 2
    along = 2 * depth + (side + depth) % 2
    step = along + (1 - plane) * (7 - 2 * along)
    return 2 * (8 * plane + step) + (core + plane + depth // 2 + step + 1) % 2


def halves(value):
    high = value.astype(jnp.bfloat16)
    return high, (value - high.astype(jnp.float32)).astype(jnp.bfloat16)


def mul(left, right):
    return jnp.dot(left, right, preferred_element_type=jnp.float32)


def ring_kernel(
    vel_hbm, eddy_hbm, op_hbm, col_hbm, plane_hbm, record_hbm, conv_hbm, speed_hbm, filter_hbm, table_hbm,
    out_ref,
    vel_ref, eddy_ref, op_ref, inlet_ref, plane_ref, record_ref, conv_ref, speed_ref, filter_ref, table_ref,
    in_sems, col_ref, rows_ref,
    vt, et, pt, state, eddy, inlets, row_vals, low, high, total, dx, sz, weights, op_cat,
    vel_send, vel_recv, eddy_send, eddy_recv, pl_send, pl_recv, row_send, row_recv,
    low_send, low_recv, high_send, high_recv, out_send, out_recv,
    eddy_via, eddy_via_recv, eddy_on, edge_send, landed,
):
    me_s, me_p = lax.axis_index("stream"), lax.axis_index("pitch")
    me = rank_of(me_s, me_p)
    home = me // 8
    offset = me % 8
    above = place_of((me + 1) % 32)
    below = place_of((me + 31) % 32)
    partner = (me_s, me_p + 1 - 2 * (me_p % 2))
    core = me_p % 2
    upper = me_s // 4
    group_upper = 1 - (me_p + 1) // 2 % 2
    feeds = (me_s == 2) | (me_s == 4)
    relays = (me_s == 3) | (me_s == 5)
    feeds_in = feeds & (group_upper != upper)
    relays_in = relays & (group_upper == upper)
    crossing = group_upper != upper
    mirrored = (me_s + 2 * (1 - upper)) % 4
    first_vel = jnp.where(crossing & (mirrored < 2), 6, 2)
    first_eddy = jnp.where(crossing & (mirrored == 1), 6, 2)
    edge = 7 * (1 - core)
    edge_peer = place_of((8 * me_p + edge + 33 - 2 * core) % 32)
    ends_low, ends_high = me % 16 == 7, me % 16 == 8
    inner = (offset >= 2) & (offset <= 5)

    def arrival(i):
        turn = jnp.where(inner, 7 - i % 4, 4 + i % 4)
        return jnp.where(i < 4, 4 * upper + i % 4, jnp.where(upper == 1, (turn + 2) % 4, turn))

    loads = [
        pltpu.make_async_copy(source, target, in_sems.at[i])
        for i, (source, target) in enumerate(
            (
                (vel_hbm, vel_ref), (plane_hbm, plane_ref), (conv_hbm, conv_ref), (speed_hbm, speed_ref),
                (eddy_hbm, eddy_ref), (filter_hbm, filter_ref), (table_hbm, table_ref), (op_hbm, op_ref),
                (col_hbm, inlet_ref), (record_hbm, record_ref),
            )
        )
    ]
    for load in loads[:4]:
        load.start()

    barrier = pltpu.get_barrier_semaphore()

    @pl.loop(1, 32)
    def _(step):
        other = (me_s * 4 + me_p + step) % 32
        pl.semaphore_signal(barrier, inc=1, device_id=(other // 4, other % 4), device_id_type=MESH_ID)

    def rows8(index):
        return pl.ds(pl.multiple_of(index * CHUNK, CHUNK), CHUNK)

    def out_copy(src, dst, send, recv, device):
        return pltpu.make_async_remote_copy(
            src_ref=src, dst_ref=dst, send_sem=send, recv_sem=recv, device_id=device,
            device_id_type=MESH_ID,
        )

    def spread_copy(kind, j):
        src, dst, send, recv = {
            "vel": (vt, state.at[0], vel_send, vel_recv),
            "eddy": (et, eddy, eddy_send, eddy_recv),
            "plane": (pt, inlets, pl_send, pl_recv),
        }[kind]
        source = src.at[pl.ds(PAIR * j, PAIR)]
        target = dst.at[me_s] if kind == "plane" else dst.at[:, rows8(me_s)]
        rank = 8 * me_p + j
        return (
            rank,
            out_copy(source, target, send.at[j], recv.at[me_s], place_of(rank)),
            lambda: pltpu.make_async_copy(source, target, recv.at[me_s]),
        )

    def spread_start(kind, j):
        rank, remote, local = spread_copy(kind, j)

        via = feeds_in & (j >= 2) & (j <= 5) if kind == "eddy" else False

        @pl.when((rank != me) & jnp.logical_not(via))
        def _():
            remote.start()

        @pl.when(rank == me)
        def _():
            local().start()

        if kind == "eddy":

            @pl.when(via)
            def _():
                k = (j + 6) % 8
                out_copy(
                    et.at[pl.ds(PAIR * j, PAIR)], eddy_via.at[k], eddy_send.at[j], eddy_via_recv.at[k],
                    (me_s + 1, me_p + 1 - 2 * core),
                ).start()

    def forward_eddy(k):
        source = (me_s + 7) % 8
        return (
            pltpu.make_async_copy(eddy_via.at[k], eddy_via.at[k], eddy_via_recv.at[k]),
            out_copy(
                eddy_via.at[k], eddy.at[:, rows8(source)], eddy_on.at[k], eddy_recv.at[source],
                place_of(8 * (me_p + 1 - 2 * core) + 2 + k),
            ),
        )

    def edge_copy(to_low):
        dst, recv = (low, low_recv) if to_low else (high, high_recv)
        return out_copy(
            vt.at[pl.ds(PAIR * edge, PAIR)], dst.at[0, :, rows8(me_s)], edge_send, recv.at[0, me_s],
            edge_peer,
        )

    def edge_start(j):
        @pl.when(crossing & (j == edge) & (core == 0))
        def _():
            edge_copy(True).start()

        @pl.when(crossing & (j == edge) & (core == 1))
        def _():
            edge_copy(False).start()

    def low_sends(n, c):
        return jnp.logical_not(ends_low & (c // 4 != upper)) if n == 0 else True

    def high_sends(n, c):
        return jnp.logical_not(ends_high & (c // 4 != upper)) if n == 0 else True

    def spread_sent(kind):
        @pl.loop(0, 8)
        def _(j):
            rank, remote, _local = spread_copy(kind, j)

            @pl.when(rank != me)
            def _():
                remote.wait_send()

    def spread_arrived(kind, s):
        src, dst, send, recv = {
            "vel": (vt, state.at[0], vel_send, vel_recv),
            "eddy": (et, eddy, eddy_send, eddy_recv),
            "plane": (pt, inlets, pl_send, pl_recv),
        }[kind]
        target = dst.at[s] if kind == "plane" else dst.at[:, rows8(s)]
        pltpu.make_async_copy(src.at[pl.ds(0, PAIR)], target, recv.at[s]).wait()

    def low_copy(n, c):
        return out_copy(
            state.at[n, :, rows8(c)], low.at[n, :, rows8(c)], low_send.at[n, c], low_recv.at[n, c], above
        )

    def high_copy(n, c):
        return out_copy(
            state.at[n, :, rows8(c)], high.at[n, :, rows8(c)], high_send.at[n, c], high_recv.at[n, c],
            below,
        )

    def result_copy(s):
        source = state.at[4, :, rows8(s)]
        target = landed.at[pl.ds(PAIR * offset, PAIR)]
        return (
            out_copy(source, target, out_send.at[s], out_recv.at[offset], (s, home)),
            lambda: pltpu.make_async_copy(source, target, out_recv.at[offset]),
        )

    loads[0].wait()
    for load in loads[4:]:
        load.start()

    pl.semaphore_wait(barrier, 31)

    @pl.loop(0, 8)
    def _(i):
        j = (i + first_vel) % 8
        for y in range(PAIR):
            vt[PAIR * j + y] = jnp.squeeze(vel_ref[:, pl.ds(PAIR * j + y, 1), :], axis=1)
        spread_start("vel", j)
        edge_start(j)

    def column_of(row):
        count = row.shape[1]
        own = lax.broadcasted_iota(jnp.int32, (count, count), 0) == lax.broadcasted_iota(
            jnp.int32, (count, count), 1
        )
        picked = jnp.sum(jnp.where(own, jnp.broadcast_to(row, (count, count)), 0.0), axis=1, keepdims=True)
        return jnp.broadcast_to(picked, (count, 128))

    for load in loads[1:4]:
        load.wait()
    rows_ref[0] = column_of(conv_ref[...])
    rows_ref[1] = column_of(speed_ref[...])
    for part in range(8):
        pt_part = plane_ref[0, :, 128 * part : 128 * part + 128]
        for y in range(16):
            pt[y, part : part + 1, :] = pt_part[y : y + 1, :]

    row_copy = out_copy(rows_ref, row_vals.at[core], row_send, row_recv, partner)
    row_copy.start()
    row_vals[core] = rows_ref[...]

    @pl.loop(0, 8)
    def _(i):
        spread_start("plane", (i + me_s + 1) % 8)

    for load in loads[4:]:
        load.wait()
    kernel_row = jnp.dot(
        jnp.broadcast_to(filter_ref[...], (8, 512)), table_ref[...],
        precision=lax.Precision.HIGHEST, preferred_element_type=jnp.float32,
    )[0:1]
    rolled = pltpu.roll(jnp.broadcast_to(kernel_row, (256, 1024)), 0, 1, stride=1, stride_axis=0)
    b0, b1, b2, b3 = (rolled[:, 256 * i : 256 * i + 256] for i in range(4))
    for i, block in enumerate(
        (
            0.25 * ((b0 + b2) + (b1 + b3)),
            0.25 * ((b0 + b2) - (b1 + b3)),
            0.5 * (b0 - b2),
            0.5 * (b1 - b3),
        )
    ):
        weights[0, i], weights[1, i] = halves(block)
    op_parts = halves(op_ref[...])
    source_index = lax.broadcasted_iota(jnp.int32, (64, 192), 0)
    column = lax.broadcasted_iota(jnp.int32, (64, 192), 1)
    into_high = ((column % 64 == source_index) & (column < 128)).astype(jnp.bfloat16)
    into_low = ((column % 64 == source_index) & (column >= 128)).astype(jnp.bfloat16)
    op_cat[...] = (mul(op_parts[0], into_high) + mul(op_parts[1], into_low)).astype(jnp.bfloat16)
    col_ref[...] = column_of(inlet_ref[...])

    @pl.loop(0, 8)
    def _(i):
        c = arrival(i)
        spread_arrived("vel", c)

        @pl.when(low_sends(0, c))
        def _():
            low_copy(0, c).start()

        @pl.when(high_sends(0, c))
        def _():
            high_copy(0, c).start()

        j = (i + first_eddy) % 8
        for y in range(PAIR):
            et[PAIR * j + y] = jnp.squeeze(eddy_ref[:, pl.ds(PAIR * j + y, 1), :], axis=1)
        spread_start("eddy", j)

    @pl.when(relays_in)
    def _():
        @pl.loop(0, 4)
        def _(k):
            arrived, onward = forward_eddy(k)
            arrived.wait()
            onward.start()

    def products(n):
        for y in range(PAIR):
            up, down = halves(state[n, y])
            dx[y] = mul(op_cat[...], jnp.concatenate([up, down, up], axis=0))
        u = state[n].reshape(128, 1024)
        v0, v1, v2, v3 = (u[:, 256 * i : 256 * i + 256] for i in range(4))
        even, odd = v0 + v2, v1 + v3

        def times(value, *which):
            up, down = halves(value)
            count = value.shape[0]
            both = jnp.concatenate([up, down], axis=0)
            found = []
            for i in which:
                wide = mul(both, weights[0, i])
                found.append(wide[:count] + wide[count:] + mul(up, weights[1, i]))
            return found

        (first,) = times(even + odd, 0)
        (second,) = times(even - odd, 1)
        straight, crossed = times(jnp.concatenate([v0 - v2, v1 - v3], axis=0), 2, 3)
        diff0 = straight[:128] - crossed[128:]
        diff1 = crossed[:128] + straight[128:]
        for i, part in enumerate(
            (
                (first + second) + diff0,
                (first - second) + diff1,
                (first + second) - diff0,
                (first - second) - diff1,
            )
        ):
            sz[:, :, 256 * i : 256 * i + 256] = part.reshape(PAIR, 64, 256)

    source_core = home % 2

    def row_value(which, y):
        row = PAIR * offset + y
        value = row_vals[source_core, which, pl.ds(row, 1), :]
        return jnp.concatenate([jnp.broadcast_to(value, (8, 128))] * 8, axis=1)

    def combine(n):
        if n == 0:
            row_copy.wait_recv()

            @pl.loop(0, 8)
            def _(s):
                spread_arrived("plane", s)

        step = (0.5 * time_step, 0.5 * time_step, time_step, 0.0)[n]
        share = time_step / 6.0 * (1.0, 2.0, 2.0, 1.0)[n]
        gusts = []
        for y in range(PAIR):
            tile = inlets[record_ref[n], y]
            gusts.append(
                jnp.concatenate(
                    [jnp.broadcast_to(tile[i : i + 1], (8, 128)) for i in range(8)], axis=1
                )
            )
        conv = [row_value(0, y) for y in range(PAIR)]
        speed = [row_value(1, y) for y in range(PAIR)]

        @pl.loop(0, 8)
        def _(i):
            c = arrival(i) if n == 0 else i
            if n == 0:
                spread_arrived("eddy", c)
            low_copy(n, c).wait_recv()
            high_copy(n, c).wait_recv()
            r = rows8(c)
            column = jnp.concatenate([col_ref[r, :]] * 8, axis=1)
            rows = [low[n, 0, r], low[n, 1, r], state[n, 0, r], state[n, 1, r], high[n, 0, r], high[n, 1, r]]
            for y in range(PAIR):
                u = rows[y + 2]
                second = (
                    16.0 * (rows[y + 1] + rows[y + 3]) - (rows[y] + rows[y + 4]) - 30.0 * u
                ) * (1.0 / 12.0)
                rate = (
                    eddy[y, r] * second
                    - (conv[y] + u) * (dx[y, r] + column * gusts[y])
                    - speed[y] * sz[y, r]
                )
                if n == 0:
                    total[y, r] = u + share * rate
                    state[1, y, r] = u + step * rate
                elif n < 3:
                    total[y, r] += share * rate
                    state[n + 1, y, r] = state[0, y, r] + step * rate
                else:
                    state[4, y, r] = total[y, r] + share * rate
            if n < 3:
                low_copy(n + 1, c).start()
                high_copy(n + 1, c).start()
            else:
                remote, local = result_copy(c)
                mine = (c == me_s) & (home == me_p)

                @pl.when(jnp.logical_not(mine))
                def _():
                    remote.start()

                @pl.when(mine)
                def _():
                    local().start()

    for n in range(4):
        products(n)
        combine(n)

    @pl.when(relays_in)
    def _():
        for k in range(4):
            forward_eddy(k)[1].wait_send()

    @pl.when(crossing)
    def _():
        edge_copy(True).wait_send()

    spread_sent("vel")
    spread_sent("plane")
    spread_sent("eddy")
    row_copy.wait_send()

    @pl.loop(0, 8)
    def _(c):
        for n in range(4):

            @pl.when(low_sends(n, c))
            def _():
                low_copy(n, c).wait_send()

            @pl.when(high_sends(n, c))
            def _():
                high_copy(n, c).wait_send()

        mine = (c == me_s) & (home == me_p)

        @pl.when(jnp.logical_not(mine))
        def _():
            result_copy(c)[0].wait_send()

        pltpu.make_async_copy(
            state.at[4, :, rows8(0)], landed.at[pl.ds(PAIR * c, PAIR)], out_recv.at[c]
        ).wait()
        for y in range(PAIR):
            out_ref[:, pl.ds(PAIR * c + y, 1), :] = jnp.expand_dims(landed[PAIR * c + y], 1)


def ring_shards(
    velocity, eddy_visc, stream_op, inlet_col, planes, record, convection, span_speed, span_filter
):
    span_len = velocity.shape[2]
    half = span_len // 2
    modes = np.arange(half)[:, None]
    angle = (modes * np.arange(span_len)[None, :] % span_len) * (2.0 * np.pi / span_len)
    table = (-2.0 / span_len * modes / half * np.sin(angle)).astype(np.float32)
    f32, dma = jnp.float32, pltpu.SemaphoreType.DMA
    result = pl.pallas_call(
        ring_kernel,
        out_shape=pltpu.VMEM((8, 16, 1024), f32),
        in_specs=[pl.BlockSpec(memory_space=pltpu.HBM)] * 10,
        out_specs=pl.BlockSpec(memory_space=pltpu.VMEM),
        scratch_shapes=[
            pltpu.VMEM((8, 16, 1024), f32),
            pltpu.VMEM((8, 16, 1024), f32),
            pltpu.VMEM((64, 64), f32),
            pltpu.VMEM((1, 64), f32),
            pltpu.VMEM((1, 16, 1024), f32),
            pltpu.SMEM((4,), jnp.int32),
            pltpu.VMEM((1, 16), f32),
            pltpu.VMEM((1, 16), f32),
            pltpu.VMEM((1, 512), f32),
            pltpu.VMEM((512, 1024), f32),
            dma((10,)),
            pltpu.VMEM((64, 128), f32),
            pltpu.VMEM((2, 16, 128), f32),
            pltpu.VMEM((16, 8, 1024), f32),
            pltpu.VMEM((16, 8, 1024), f32),
            pltpu.VMEM((16, 8, 128), f32),
            pltpu.VMEM((5, 2, 64, 1024), f32),
            pltpu.VMEM((2, 64, 1024), f32),
            pltpu.VMEM((8, 2, 8, 128), f32),
            pltpu.VMEM((2, 2, 16, 128), f32),
            pltpu.VMEM((4, 2, 64, 1024), f32),
            pltpu.VMEM((4, 2, 64, 1024), f32),
            pltpu.VMEM((2, 64, 1024), f32),
            pltpu.VMEM((2, 64, 1024), f32),
            pltpu.VMEM((2, 64, 1024), f32),
            pltpu.VMEM((2, 4, 256, 256), jnp.bfloat16),
            pltpu.VMEM((64, 192), jnp.bfloat16),
            dma((8,)), dma((8,)), dma((8,)), dma((8,)), dma((8,)), dma((8,)), dma, dma,
            dma((4, 8)), dma((4, 8)), dma((4, 8)), dma((4, 8)), dma((8,)), dma((8,)),
            pltpu.VMEM((4, 2, 8, 1024), f32), dma((4,)), dma((4,)), dma,
            pltpu.VMEM((16, 8, 1024), f32),
        ],
        compiler_params=pltpu.CompilerParams(
            collective_id=0, has_side_effects=True, vmem_limit_bytes=56 * 2**20
        ),
    )(
        velocity,
        eddy_visc,
        stream_op,
        inlet_col[None, :],
        planes,
        record,
        convection[None, :],
        span_speed[None, :],
        span_filter[None, :],
        jnp.asarray(table),
    )
    return result


def either(velocity, *others):
    fits = (
        lax.axis_size("stream") == 8
        and lax.axis_size("pitch") == 4
        and velocity.shape == (8, 16, 1024)
    )
    return (ring_shards if fits else shards)(velocity, *others)


def solution(mesh):
    placed = (
        P("stream", "pitch", None),
        P("stream", "pitch", None),
        P(),
        P(),
        P("stream", "pitch", None),
        P(),
        P("pitch"),
        P("pitch"),
        P(),
    )
    return jax.shard_map(
        either, mesh=mesh, in_specs=placed, out_specs=P("stream", "pitch", None), check_vma=False
    )
```

```python
import math

import jax
import jax.numpy as jnp
import numpy as np
from jax import lax
from jax.experimental import pallas as pl
from jax.experimental.pallas import tpu as pltpu
from jax.sharding import PartitionSpec as P

time_step = 0.25


def spread(shard, axis, root):
    mine = lax.axis_index(axis) == root
    return lax.psum(jnp.where(mine, shard, jnp.zeros_like(shard)), axis)


def with_halo(shard, sides, width):
    for axis, dim in sides:
        peers, length = (lax.axis_size(axis), shard.shape[dim])
        up = [(i, (i + 1) % peers) for i in range(peers)]
        down = [(j, i) for i, j in up]
        last = lax.slice_in_dim(shard, length - width, length, axis=dim)
        initial = lax.slice_in_dim(shard, 0, width, axis=dim)
        before = lax.ppermute(last, axis, up)
        after = lax.ppermute(initial, axis, down)
        shard = jnp.concatenate([before, shard, after], axis=dim)
    return shard


def pitch_second(padded):
    return (
        -padded[:, 0:-4]
        + 16.0 * padded[:, 1:-3]
        - 30.0 * padded[:, 2:-2]
        + 16.0 * padded[:, 3:-1]
        - padded[:, 4:]
    ) / 12.0


def shards(
    velocity, eddy_visc, stream_op, inlet_col, planes, record, convection, span_speed, span_filter
):
    cells_x, cells_y, span_len = velocity.shape
    stream_len = stream_op.shape[0]
    span_piece = span_len // lax.axis_size("stream")
    position = lax.axis_index("stream")
    half = span_len // 2
    rows_index = lax.iota(jnp.int32, span_len)[:, None]
    mode_index = lax.iota(jnp.int32, half)[None, :]
    angle = (rows_index * mode_index % span_len).astype(jnp.float32) * (2.0 * math.pi / span_len)
    table_dft = jnp.concatenate([jnp.cos(angle), jnp.sin(angle)], axis=1)
    gains = span_filter * lax.iota(jnp.float32, half) / half
    conv_rows = convection[None, :, None]
    span_rows = span_speed[None, :, None]

    def inlet_at(section):
        whole = spread(planes[0], "stream", record[section])
        return lax.dynamic_slice_in_dim(whole, position * span_piece, span_piece, 1)

    def span_part(state):
        flat = state.reshape(-1, span_len)
        coeffs = jnp.dot(
            flat, table_dft, precision=lax.Precision.HIGHEST, preferred_element_type=jnp.float32
        )
        mixed = jnp.concatenate([coeffs[:, half:] * gains, -coeffs[:, :half] * gains], axis=1)
        back = lax.dot_general(
            mixed,
            table_dft,
            (((1,), (1,)), ((), ())),
            precision=lax.Precision.HIGHEST,
            preferred_element_type=jnp.float32,
        )
        return (back * (2.0 / span_len)).reshape(state.shape)

    def section_rate(state, section):
        inlet_slice = inlet_at(section)
        pencil = lax.all_to_all(state, "stream", split_axis=2, concat_axis=0, tiled=True)
        stream_deriv = jnp.dot(
            stream_op,
            pencil.reshape(stream_len, -1),
            precision=lax.Precision.HIGHEST,
            preferred_element_type=jnp.float32,
        )
        stream_deriv = (
            stream_deriv.reshape(pencil.shape) + inlet_col[:, None, None] * inlet_slice[None, :, :]
        )
        returned = lax.all_to_all(stream_deriv, "stream", split_axis=0, concat_axis=2, tiled=True)
        padded = with_halo(state, (("pitch", 1),), 2)
        local_terms = -(conv_rows + state) * returned + eddy_visc * pitch_second(padded)
        return local_terms - span_rows * span_part(state)

    first = section_rate(velocity, 0)
    second = section_rate(velocity + 0.5 * time_step * first, 1)
    third = section_rate(velocity + 0.5 * time_step * second, 2)
    fourth = section_rate(velocity + time_step * third, 3)
    return velocity + time_step / 6.0 * (first + 2.0 * second + 2.0 * third + fourth)


CHUNK = 8
PAIR = 2
MESH_ID = pl.DeviceIdType.MESH


def place_of(rank):
    spot, turn = rank // 2, rank % 2
    plane, step = spot // 8, spot % 8
    along = step + (1 - plane) * (7 - 2 * step)
    depth = along // 2
    core = (plane + depth // 2 + step + turn + 1) % 2
    return 2 * depth + (along + 1) // 2 % 2, 2 * plane + core


def rank_of(stream, pitch):
    depth, side, plane, core = stream // 2, stream % 2, pitch // 2, pitch % 2
    along = 2 * depth + (side + depth) % 2
    step = along + (1 - plane) * (7 - 2 * along)
    return 2 * (8 * plane + step) + (core + plane + depth // 2 + step + 1) % 2


def halves(value):
    high = value.astype(jnp.bfloat16)
    return high, (value - high.astype(jnp.float32)).astype(jnp.bfloat16)


def mul(left, right):
    return jnp.dot(left, right, preferred_element_type=jnp.float32)


def ring_kernel(
    vel_hbm, eddy_hbm, op_hbm, col_hbm, plane_hbm, record_hbm, conv_hbm, speed_hbm, filter_hbm, table_hbm,
    out_ref,
    vel_ref, eddy_ref, op_ref, inlet_ref, plane_ref, record_ref, conv_ref, speed_ref, filter_ref, table_ref,
    in_sems, col_ref, rows_ref,
    vt, et, pt, state, eddy, inlets, row_vals, low, high, total, dx, sz, weights, op_cat,
    vel_send, vel_recv, eddy_send, eddy_recv, pl_send, pl_recv, row_send, row_recv,
    low_send, low_recv, high_send, high_recv, out_send, out_recv,
    eddy_via, eddy_via_recv, eddy_on, edge_send, landed,
):
    me_s, me_p = lax.axis_index("stream"), lax.axis_index("pitch")
    me = rank_of(me_s, me_p)
    home = me // 8
    offset = me % 8
    above = place_of((me + 1) % 32)
    below = place_of((me + 31) % 32)
    partner = (me_s, me_p + 1 - 2 * (me_p % 2))
    core = me_p % 2
    upper = me_s // 4
    group_upper = 1 - (me_p + 1) // 2 % 2
    feeds = (me_s == 2) | (me_s == 4)
    relays = (me_s == 3) | (me_s == 5)
    feeds_in = feeds & (group_upper != upper)
    relays_in = relays & (group_upper == upper)
    crossing = group_upper != upper
    mirrored = (me_s + 2 * (1 - upper)) % 4
    first_vel = jnp.where(crossing & (mirrored < 2), 6, 2)
    first_eddy = jnp.where(crossing & (mirrored == 1), 6, 2)
    edge = 7 * (1 - core)
    edge_peer = place_of((8 * me_p + edge + 33 - 2 * core) % 32)
    ends_low, ends_high = me % 16 == 7, me % 16 == 8
    inner = (offset >= 2) & (offset <= 5)

    def arrival(i):
        turn = jnp.where(inner, 7 - i % 4, 4 + i % 4)
        return jnp.where(i < 4, 4 * upper + i % 4, jnp.where(upper == 1, (turn + 2) % 4, turn))

    loads = [
        pltpu.make_async_copy(source, target, in_sems.at[i])
        for i, (source, target) in enumerate(
            (
                (vel_hbm, vel_ref), (plane_hbm, plane_ref), (conv_hbm, conv_ref), (speed_hbm, speed_ref),
                (eddy_hbm, eddy_ref), (filter_hbm, filter_ref), (table_hbm, table_ref), (op_hbm, op_ref),
                (col_hbm, inlet_ref), (record_hbm, record_ref),
            )
        )
    ]
    for load in loads[:4]:
        load.start()

    barrier = pltpu.get_barrier_semaphore()

    @pl.loop(1, 32)
    def _(step):
        other = (me_s * 4 + me_p + step) % 32
        pl.semaphore_signal(barrier, inc=1, device_id=(other // 4, other % 4), device_id_type=MESH_ID)

    def rows8(index):
        return pl.ds(pl.multiple_of(index * CHUNK, CHUNK), CHUNK)

    def out_copy(src, dst, send, recv, device):
        return pltpu.make_async_remote_copy(
            src_ref=src, dst_ref=dst, send_sem=send, recv_sem=recv, device_id=device,
            device_id_type=MESH_ID,
        )

    def spread_copy(kind, j):
        src, dst, send, recv = {
            "vel": (vt, state.at[0], vel_send, vel_recv),
            "eddy": (et, eddy, eddy_send, eddy_recv),
            "plane": (pt, inlets, pl_send, pl_recv),
        }[kind]
        source = src.at[pl.ds(PAIR * j, PAIR)]
        target = dst.at[me_s] if kind == "plane" else dst.at[:, rows8(me_s)]
        rank = 8 * me_p + j
        return (
            rank,
            out_copy(source, target, send.at[j], recv.at[me_s], place_of(rank)),
            lambda: pltpu.make_async_copy(source, target, recv.at[me_s]),
        )

    def spread_start(kind, j):
        rank, remote, local = spread_copy(kind, j)

        via = feeds_in & (j >= 2) & (j <= 5) if kind == "eddy" else False

        @pl.when((rank != me) & jnp.logical_not(via))
        def _():
            remote.start()

        @pl.when(rank == me)
        def _():
            local().start()

        if kind == "eddy":

            @pl.when(via)
            def _():
                k = (j + 6) % 8
                out_copy(
                    et.at[pl.ds(PAIR * j, PAIR)], eddy_via.at[k], eddy_send.at[j], eddy_via_recv.at[k],
                    (me_s + 1, me_p + 1 - 2 * core),
                ).start()

    def forward_eddy(k):
        source = (me_s + 7) % 8
        return (
            pltpu.make_async_copy(eddy_via.at[k], eddy_via.at[k], eddy_via_recv.at[k]),
            out_copy(
                eddy_via.at[k], eddy.at[:, rows8(source)], eddy_on.at[k], eddy_recv.at[source],
                place_of(8 * (me_p + 1 - 2 * core) + 2 + k),
            ),
        )

    def edge_copy(to_low):
        dst, recv = (low, low_recv) if to_low else (high, high_recv)
        return out_copy(
            vt.at[pl.ds(PAIR * edge, PAIR)], dst.at[0, :, rows8(me_s)], edge_send, recv.at[0, me_s],
            edge_peer,
        )

    def edge_start(j):
        @pl.when(crossing & (j == edge) & (core == 0))
        def _():
            edge_copy(True).start()

        @pl.when(crossing & (j == edge) & (core == 1))
        def _():
            edge_copy(False).start()

    def low_sends(n, c):
        return jnp.logical_not(ends_low & (c // 4 != upper)) if n == 0 else True

    def high_sends(n, c):
        return jnp.logical_not(ends_high & (c // 4 != upper)) if n == 0 else True

    def spread_sent(kind):
        @pl.loop(0, 8)
        def _(j):
            rank, remote, _local = spread_copy(kind, j)

            @pl.when(rank != me)
            def _():
                remote.wait_send()

    def spread_arrived(kind, s):
        src, dst, send, recv = {
            "vel": (vt, state.at[0], vel_send, vel_recv),
            "eddy": (et, eddy, eddy_send, eddy_recv),
            "plane": (pt, inlets, pl_send, pl_recv),
        }[kind]
        target = dst.at[s] if kind == "plane" else dst.at[:, rows8(s)]
        pltpu.make_async_copy(src.at[pl.ds(0, PAIR)], target, recv.at[s]).wait()

    def low_copy(n, c):
        return out_copy(
            state.at[n, :, rows8(c)], low.at[n, :, rows8(c)], low_send.at[n, c], low_recv.at[n, c], above
        )

    def high_copy(n, c):
        return out_copy(
            state.at[n, :, rows8(c)], high.at[n, :, rows8(c)], high_send.at[n, c], high_recv.at[n, c],
            below,
        )

    def result_copy(s):
        source = state.at[4, :, rows8(s)]
        target = landed.at[pl.ds(PAIR * offset, PAIR)]
        return (
            out_copy(source, target, out_send.at[s], out_recv.at[offset], (s, home)),
            lambda: pltpu.make_async_copy(source, target, out_recv.at[offset]),
        )

    loads[0].wait()
    for load in loads[4:]:
        load.start()

    pl.semaphore_wait(barrier, 31)

    @pl.loop(0, 8)
    def _(i):
        j = (i + first_vel) % 8
        for y in range(PAIR):
            vt[PAIR * j + y] = jnp.squeeze(vel_ref[:, pl.ds(PAIR * j + y, 1), :], axis=1)
        spread_start("vel", j)
        edge_start(j)

    def column_of(row):
        count = row.shape[1]
        own = lax.broadcasted_iota(jnp.int32, (count, count), 0) == lax.broadcasted_iota(
            jnp.int32, (count, count), 1
        )
        picked = jnp.sum(jnp.where(own, jnp.broadcast_to(row, (count, count)), 0.0), axis=1, keepdims=True)
        return jnp.broadcast_to(picked, (count, 128))

    for load in loads[1:4]:
        load.wait()
    rows_ref[0] = column_of(conv_ref[...])
    rows_ref[1] = column_of(speed_ref[...])
    for part in range(8):
        pt_part = plane_ref[0, :, 128 * part : 128 * part + 128]
        for y in range(16):
            pt[y, part : part + 1, :] = pt_part[y : y + 1, :]

    row_copy = out_copy(rows_ref, row_vals.at[core], row_send, row_recv, partner)
    row_copy.start()
    row_vals[core] = rows_ref[...]

    @pl.loop(0, 8)
    def _(i):
        spread_start("plane", (i + me_s + 1) % 8)

    for load in loads[4:]:
        load.wait()
    kernel_row = jnp.dot(
        jnp.broadcast_to(filter_ref[...], (8, 512)), table_ref[...],
        precision=lax.Precision.HIGHEST, preferred_element_type=jnp.float32,
    )[0:1]
    rolled = pltpu.roll(jnp.broadcast_to(kernel_row, (256, 1024)), 0, 1, stride=1, stride_axis=0)
    b0, b1, b2, b3 = (rolled[:, 256 * i : 256 * i + 256] for i in range(4))
    for i, block in enumerate(
        (
            0.25 * ((b0 + b2) + (b1 + b3)),
            0.25 * ((b0 + b2) - (b1 + b3)),
            0.5 * (b0 - b2),
            0.5 * (b1 - b3),
        )
    ):
        weights[0, i], weights[1, i] = halves(block)
    op_parts = halves(op_ref[...])
    source_index = lax.broadcasted_iota(jnp.int32, (64, 192), 0)
    column = lax.broadcasted_iota(jnp.int32, (64, 192), 1)
    into_high = ((column % 64 == source_index) & (column < 128)).astype(jnp.bfloat16)
    into_low = ((column % 64 == source_index) & (column >= 128)).astype(jnp.bfloat16)
    op_cat[...] = (mul(op_parts[0], into_high) + mul(op_parts[1], into_low)).astype(jnp.bfloat16)
    col_ref[...] = column_of(inlet_ref[...])

    @pl.loop(0, 8)
    def _(i):
        j = (i + first_eddy) % 8
        for y in range(PAIR):
            et[PAIR * j + y] = jnp.squeeze(eddy_ref[:, pl.ds(PAIR * j + y, 1), :], axis=1)
        spread_start("eddy", j)

    @pl.loop(0, 8)
    def _(i):
        c = arrival(i)
        spread_arrived("vel", c)

        @pl.when(low_sends(0, c))
        def _():
            low_copy(0, c).start()

        @pl.when(high_sends(0, c))
        def _():
            high_copy(0, c).start()

    @pl.when(relays_in)
    def _():
        @pl.loop(0, 4)
        def _(k):
            arrived, onward = forward_eddy(k)
            arrived.wait()
            onward.start()

    def products(n):
        for y in range(PAIR):
            up, down = halves(state[n, y])
            dx[y] = mul(op_cat[...], jnp.concatenate([up, down, up], axis=0))
        u = state[n].reshape(128, 1024)
        v0, v1, v2, v3 = (u[:, 256 * i : 256 * i + 256] for i in range(4))
        even, odd = v0 + v2, v1 + v3

        def times(value, *which):
            up, down = halves(value)
            count = value.shape[0]
            both = jnp.concatenate([up, down], axis=0)
            found = []
            for i in which:
                wide = mul(both, weights[0, i])
                found.append(wide[:count] + wide[count:] + mul(up, weights[1, i]))
            return found

        (first,) = times(even + odd, 0)
        (second,) = times(even - odd, 1)
        straight, crossed = times(jnp.concatenate([v0 - v2, v1 - v3], axis=0), 2, 3)
        diff0 = straight[:128] - crossed[128:]
        diff1 = crossed[:128] + straight[128:]
        for i, part in enumerate(
            (
                (first + second) + diff0,
                (first - second) + diff1,
                (first + second) - diff0,
                (first - second) - diff1,
            )
        ):
            sz[:, :, 256 * i : 256 * i + 256] = part.reshape(PAIR, 64, 256)

    source_core = home % 2

    def row_value(which, y):
        row = PAIR * offset + y
        value = row_vals[source_core, which, pl.ds(row, 1), :]
        return jnp.concatenate([jnp.broadcast_to(value, (8, 128))] * 8, axis=1)

    def combine(n):
        if n == 0:
            row_copy.wait_recv()

            @pl.loop(0, 8)
            def _(s):
                spread_arrived("plane", s)

        step = (0.5 * time_step, 0.5 * time_step, time_step, 0.0)[n]
        share = time_step / 6.0 * (1.0, 2.0, 2.0, 1.0)[n]
        gusts = []
        for y in range(PAIR):
            tile = inlets[record_ref[n], y]
            gusts.append(
                jnp.concatenate(
                    [jnp.broadcast_to(tile[i : i + 1], (8, 128)) for i in range(8)], axis=1
                )
            )
        conv = [row_value(0, y) for y in range(PAIR)]
        speed = [row_value(1, y) for y in range(PAIR)]

        @pl.loop(0, 8)
        def _(i):
            c = arrival(i) if n == 0 else i
            if n == 0:
                spread_arrived("eddy", c)
            low_copy(n, c).wait_recv()
            high_copy(n, c).wait_recv()
            r = rows8(c)
            column = jnp.concatenate([col_ref[r, :]] * 8, axis=1)
            rows = [low[n, 0, r], low[n, 1, r], state[n, 0, r], state[n, 1, r], high[n, 0, r], high[n, 1, r]]
            for y in range(PAIR):
                u = rows[y + 2]
                second = (
                    16.0 * (rows[y + 1] + rows[y + 3]) - (rows[y] + rows[y + 4]) - 30.0 * u
                ) * (1.0 / 12.0)
                rate = (
                    eddy[y, r] * second
                    - (conv[y] + u) * (dx[y, r] + column * gusts[y])
                    - speed[y] * sz[y, r]
                )
                if n == 0:
                    total[y, r] = u + share * rate
                    state[1, y, r] = u + step * rate
                elif n < 3:
                    total[y, r] += share * rate
                    state[n + 1, y, r] = state[0, y, r] + step * rate
                else:
                    state[4, y, r] = total[y, r] + share * rate
            if n < 3:
                low_copy(n + 1, c).start()
                high_copy(n + 1, c).start()
            else:
                remote, local = result_copy(c)
                mine = (c == me_s) & (home == me_p)

                @pl.when(jnp.logical_not(mine))
                def _():
                    remote.start()

                @pl.when(mine)
                def _():
                    local().start()

    for n in range(4):
        products(n)
        combine(n)

    @pl.when(relays_in)
    def _():
        for k in range(4):
            forward_eddy(k)[1].wait_send()

    @pl.when(crossing)
    def _():
        edge_copy(True).wait_send()

    spread_sent("vel")
    spread_sent("plane")
    spread_sent("eddy")
    row_copy.wait_send()

    @pl.loop(0, 8)
    def _(c):
        for n in range(4):

            @pl.when(low_sends(n, c))
            def _():
                low_copy(n, c).wait_send()

            @pl.when(high_sends(n, c))
            def _():
                high_copy(n, c).wait_send()

        mine = (c == me_s) & (home == me_p)

        @pl.when(jnp.logical_not(mine))
        def _():
            result_copy(c)[0].wait_send()

        pltpu.make_async_copy(
            state.at[4, :, rows8(0)], landed.at[pl.ds(PAIR * c, PAIR)], out_recv.at[c]
        ).wait()
        for y in range(PAIR):
            out_ref[:, pl.ds(PAIR * c + y, 1), :] = jnp.expand_dims(landed[PAIR * c + y], 1)


def ring_shards(
    velocity, eddy_visc, stream_op, inlet_col, planes, record, convection, span_speed, span_filter
):
    span_len = velocity.shape[2]
    half = span_len // 2
    modes = np.arange(half)[:, None]
    angle = (modes * np.arange(span_len)[None, :] % span_len) * (2.0 * np.pi / span_len)
    table = (-2.0 / span_len * modes / half * np.sin(angle)).astype(np.float32)
    f32, dma = jnp.float32, pltpu.SemaphoreType.DMA
    result = pl.pallas_call(
        ring_kernel,
        out_shape=pltpu.VMEM((8, 16, 1024), f32),
        in_specs=[pl.BlockSpec(memory_space=pltpu.HBM)] * 10,
        out_specs=pl.BlockSpec(memory_space=pltpu.VMEM),
        scratch_shapes=[
            pltpu.VMEM((8, 16, 1024), f32),
            pltpu.VMEM((8, 16, 1024), f32),
            pltpu.VMEM((64, 64), f32),
            pltpu.VMEM((1, 64), f32),
            pltpu.VMEM((1, 16, 1024), f32),
            pltpu.SMEM((4,), jnp.int32),
            pltpu.VMEM((1, 16), f32),
            pltpu.VMEM((1, 16), f32),
            pltpu.VMEM((1, 512), f32),
            pltpu.VMEM((512, 1024), f32),
            dma((10,)),
            pltpu.VMEM((64, 128), f32),
            pltpu.VMEM((2, 16, 128), f32),
            pltpu.VMEM((16, 8, 1024), f32),
            pltpu.VMEM((16, 8, 1024), f32),
            pltpu.VMEM((16, 8, 128), f32),
            pltpu.VMEM((5, 2, 64, 1024), f32),
            pltpu.VMEM((2, 64, 1024), f32),
            pltpu.VMEM((8, 2, 8, 128), f32),
            pltpu.VMEM((2, 2, 16, 128), f32),
            pltpu.VMEM((4, 2, 64, 1024), f32),
            pltpu.VMEM((4, 2, 64, 1024), f32),
            pltpu.VMEM((2, 64, 1024), f32),
            pltpu.VMEM((2, 64, 1024), f32),
            pltpu.VMEM((2, 64, 1024), f32),
            pltpu.VMEM((2, 4, 256, 256), jnp.bfloat16),
            pltpu.VMEM((64, 192), jnp.bfloat16),
            dma((8,)), dma((8,)), dma((8,)), dma((8,)), dma((8,)), dma((8,)), dma, dma,
            dma((4, 8)), dma((4, 8)), dma((4, 8)), dma((4, 8)), dma((8,)), dma((8,)),
            pltpu.VMEM((4, 2, 8, 1024), f32), dma((4,)), dma((4,)), dma,
            pltpu.VMEM((16, 8, 1024), f32),
        ],
        compiler_params=pltpu.CompilerParams(
            collective_id=0, has_side_effects=True, vmem_limit_bytes=56 * 2**20
        ),
    )(
        velocity,
        eddy_visc,
        stream_op,
        inlet_col[None, :],
        planes,
        record,
        convection[None, :],
        span_speed[None, :],
        span_filter[None, :],
        jnp.asarray(table),
    )
    return result


def either(velocity, *others):
    fits = (
        lax.axis_size("stream") == 8
        and lax.axis_size("pitch") == 4
        and velocity.shape == (8, 16, 1024)
    )
    return (ring_shards if fits else shards)(velocity, *others)


def solution(mesh):
    placed = (
        P("stream", "pitch", None),
        P("stream", "pitch", None),
        P(),
        P(),
        P("stream", "pitch", None),
        P(),
        P("pitch"),
        P("pitch"),
        P(),
    )
    return jax.shard_map(
        either, mesh=mesh, in_specs=placed, out_specs=P("stream", "pitch", None), check_vma=False
    )
```

```python
import math

import jax
import jax.numpy as jnp
import numpy as np
from jax import lax
from jax.experimental import pallas as pl
from jax.experimental.pallas import tpu as pltpu
from jax.sharding import PartitionSpec as P

time_step = 0.25


def spread(shard, axis, root):
    mine = lax.axis_index(axis) == root
    return lax.psum(jnp.where(mine, shard, jnp.zeros_like(shard)), axis)


def with_halo(shard, sides, width):
    for axis, dim in sides:
        peers, length = (lax.axis_size(axis), shard.shape[dim])
        up = [(i, (i + 1) % peers) for i in range(peers)]
        down = [(j, i) for i, j in up]
        last = lax.slice_in_dim(shard, length - width, length, axis=dim)
        initial = lax.slice_in_dim(shard, 0, width, axis=dim)
        before = lax.ppermute(last, axis, up)
        after = lax.ppermute(initial, axis, down)
        shard = jnp.concatenate([before, shard, after], axis=dim)
    return shard


def pitch_second(padded):
    return (
        -padded[:, 0:-4]
        + 16.0 * padded[:, 1:-3]
        - 30.0 * padded[:, 2:-2]
        + 16.0 * padded[:, 3:-1]
        - padded[:, 4:]
    ) / 12.0


def shards(
    velocity, eddy_visc, stream_op, inlet_col, planes, record, convection, span_speed, span_filter
):
    cells_x, cells_y, span_len = velocity.shape
    stream_len = stream_op.shape[0]
    span_piece = span_len // lax.axis_size("stream")
    position = lax.axis_index("stream")
    half = span_len // 2
    rows_index = lax.iota(jnp.int32, span_len)[:, None]
    mode_index = lax.iota(jnp.int32, half)[None, :]
    angle = (rows_index * mode_index % span_len).astype(jnp.float32) * (2.0 * math.pi / span_len)
    table_dft = jnp.concatenate([jnp.cos(angle), jnp.sin(angle)], axis=1)
    gains = span_filter * lax.iota(jnp.float32, half) / half
    conv_rows = convection[None, :, None]
    span_rows = span_speed[None, :, None]

    def inlet_at(section):
        whole = spread(planes[0], "stream", record[section])
        return lax.dynamic_slice_in_dim(whole, position * span_piece, span_piece, 1)

    def span_part(state):
        flat = state.reshape(-1, span_len)
        coeffs = jnp.dot(
            flat, table_dft, precision=lax.Precision.HIGHEST, preferred_element_type=jnp.float32
        )
        mixed = jnp.concatenate([coeffs[:, half:] * gains, -coeffs[:, :half] * gains], axis=1)
        back = lax.dot_general(
            mixed,
            table_dft,
            (((1,), (1,)), ((), ())),
            precision=lax.Precision.HIGHEST,
            preferred_element_type=jnp.float32,
        )
        return (back * (2.0 / span_len)).reshape(state.shape)

    def section_rate(state, section):
        inlet_slice = inlet_at(section)
        pencil = lax.all_to_all(state, "stream", split_axis=2, concat_axis=0, tiled=True)
        stream_deriv = jnp.dot(
            stream_op,
            pencil.reshape(stream_len, -1),
            precision=lax.Precision.HIGHEST,
            preferred_element_type=jnp.float32,
        )
        stream_deriv = (
            stream_deriv.reshape(pencil.shape) + inlet_col[:, None, None] * inlet_slice[None, :, :]
        )
        returned = lax.all_to_all(stream_deriv, "stream", split_axis=0, concat_axis=2, tiled=True)
        padded = with_halo(state, (("pitch", 1),), 2)
        local_terms = -(conv_rows + state) * returned + eddy_visc * pitch_second(padded)
        return local_terms - span_rows * span_part(state)

    first = section_rate(velocity, 0)
    second = section_rate(velocity + 0.5 * time_step * first, 1)
    third = section_rate(velocity + 0.5 * time_step * second, 2)
    fourth = section_rate(velocity + time_step * third, 3)
    return velocity + time_step / 6.0 * (first + 2.0 * second + 2.0 * third + fourth)


CHUNK = 8
PAIR = 2
MESH_ID = pl.DeviceIdType.MESH


def place_of(rank):
    spot, turn = rank // 2, rank % 2
    plane, step = spot // 8, spot % 8
    along = step + (1 - plane) * (7 - 2 * step)
    depth = along // 2
    core = (plane + depth // 2 + step + turn + 1) % 2
    return 2 * depth + (along + 1) // 2 % 2, 2 * plane + core


def rank_of(stream, pitch):
    depth, side, plane, core = stream // 2, stream % 2, pitch // 2, pitch % 2
    along = 2 * depth + (side + depth) % 2
    step = along + (1 - plane) * (7 - 2 * along)
    return 2 * (8 * plane + step) + (core + plane + depth // 2 + step + 1) % 2


def halves(value):
    high = value.astype(jnp.bfloat16)
    return high, (value - high.astype(jnp.float32)).astype(jnp.bfloat16)


def mul(left, right):
    return jnp.dot(left, right, preferred_element_type=jnp.float32)


def ring_kernel(
    vel_hbm, eddy_hbm, op_hbm, col_hbm, plane_hbm, record_hbm, conv_hbm, speed_hbm, filter_hbm, table_hbm,
    out_ref,
    vel_ref, eddy_ref, op_ref, inlet_ref, plane_ref, record_ref, conv_ref, speed_ref, filter_ref, table_ref,
    in_sems, col_ref, rows_ref,
    vt, et, pt, state, eddy, inlets, row_vals, low, high, total, dx, sz, weights, op_cat,
    vel_send, vel_recv, eddy_send, eddy_recv, pl_send, pl_recv, row_send, row_recv,
    low_send, low_recv, high_send, high_recv, out_send, out_recv,
    eddy_via, eddy_via_recv, eddy_on, edge_send, landed,
):
    me_s, me_p = lax.axis_index("stream"), lax.axis_index("pitch")
    me = rank_of(me_s, me_p)
    home = me // 8
    offset = me % 8
    above = place_of((me + 1) % 32)
    below = place_of((me + 31) % 32)
    partner = (me_s, me_p + 1 - 2 * (me_p % 2))
    core = me_p % 2
    upper = me_s // 4
    group_upper = 1 - (me_p + 1) // 2 % 2
    feeds = (me_s == 2) | (me_s == 4)
    relays = (me_s == 3) | (me_s == 5)
    feeds_in = feeds & (group_upper != upper)
    relays_in = relays & (group_upper == upper)
    crossing = group_upper != upper
    mirrored = (me_s + 2 * (1 - upper)) % 4
    first_vel = jnp.where(crossing & (mirrored < 2), 6, 2)
    first_eddy = jnp.where(crossing & (mirrored == 1), 6, 2)
    edge = 7 * (1 - core)
    edge_peer = place_of((8 * me_p + edge + 33 - 2 * core) % 32)
    ends_low, ends_high = me % 16 == 7, me % 16 == 8
    inner = (offset >= 2) & (offset <= 5)

    def arrival(i):
        turn = jnp.where(inner, 7 - i % 4, 4 + i % 4)
        return jnp.where(i < 4, 4 * upper + i % 4, jnp.where(upper == 1, (turn + 2) % 4, turn))

    loads = [
        pltpu.make_async_copy(source, target, in_sems.at[i])
        for i, (source, target) in enumerate(
            (
                (vel_hbm, vel_ref), (plane_hbm, plane_ref), (conv_hbm, conv_ref), (speed_hbm, speed_ref),
                (eddy_hbm, eddy_ref), (filter_hbm, filter_ref), (table_hbm, table_ref), (op_hbm, op_ref),
                (col_hbm, inlet_ref), (record_hbm, record_ref),
            )
        )
    ]
    for load in loads[:4]:
        load.start()

    barrier = pltpu.get_barrier_semaphore()

    @pl.loop(1, 32)
    def _(step):
        other = (me_s * 4 + me_p + step) % 32
        pl.semaphore_signal(barrier, inc=1, device_id=(other // 4, other % 4), device_id_type=MESH_ID)

    def rows8(index):
        return pl.ds(pl.multiple_of(index * CHUNK, CHUNK), CHUNK)

    def out_copy(src, dst, send, recv, device):
        return pltpu.make_async_remote_copy(
            src_ref=src, dst_ref=dst, send_sem=send, recv_sem=recv, device_id=device,
            device_id_type=MESH_ID,
        )

    def spread_copy(kind, j):
        src, dst, send, recv = {
            "vel": (vt, state.at[0], vel_send, vel_recv),
            "eddy": (et, eddy, eddy_send, eddy_recv),
            "plane": (pt, inlets, pl_send, pl_recv),
        }[kind]
        source = src.at[pl.ds(PAIR * j, PAIR)]
        target = dst.at[me_s] if kind == "plane" else dst.at[:, rows8(me_s)]
        rank = 8 * me_p + j
        return (
            rank,
            out_copy(source, target, send.at[j], recv.at[me_s], place_of(rank)),
            lambda: pltpu.make_async_copy(source, target, recv.at[me_s]),
        )

    def spread_start(kind, j):
        rank, remote, local = spread_copy(kind, j)

        via = feeds_in & (j >= 2) & (j <= 5) if kind == "eddy" else False

        @pl.when((rank != me) & jnp.logical_not(via))
        def _():
            remote.start()

        @pl.when(rank == me)
        def _():
            local().start()

        if kind == "eddy":

            @pl.when(via)
            def _():
                k = (j + 6) % 8
                out_copy(
                    et.at[pl.ds(PAIR * j, PAIR)], eddy_via.at[k], eddy_send.at[j], eddy_via_recv.at[k],
                    (me_s + 1, me_p + 1 - 2 * core),
                ).start()

    def forward_eddy(k):
        source = (me_s + 7) % 8
        return (
            pltpu.make_async_copy(eddy_via.at[k], eddy_via.at[k], eddy_via_recv.at[k]),
            out_copy(
                eddy_via.at[k], eddy.at[:, rows8(source)], eddy_on.at[k], eddy_recv.at[source],
                place_of(8 * (me_p + 1 - 2 * core) + 2 + k),
            ),
        )

    def edge_copy(to_low):
        dst, recv = (low, low_recv) if to_low else (high, high_recv)
        return out_copy(
            vt.at[pl.ds(PAIR * edge, PAIR)], dst.at[0, :, rows8(me_s)], edge_send, recv.at[0, me_s],
            edge_peer,
        )

    def edge_start(j):
        @pl.when(crossing & (j == edge) & (core == 0))
        def _():
            edge_copy(True).start()

        @pl.when(crossing & (j == edge) & (core == 1))
        def _():
            edge_copy(False).start()

    def low_sends(n, c):
        return jnp.logical_not(ends_low & (c // 4 != upper)) if n == 0 else True

    def high_sends(n, c):
        return jnp.logical_not(ends_high & (c // 4 != upper)) if n == 0 else True

    def spread_sent(kind):
        @pl.loop(0, 8)
        def _(j):
            rank, remote, _local = spread_copy(kind, j)

            @pl.when(rank != me)
            def _():
                remote.wait_send()

    def spread_arrived(kind, s):
        src, dst, send, recv = {
            "vel": (vt, state.at[0], vel_send, vel_recv),
            "eddy": (et, eddy, eddy_send, eddy_recv),
            "plane": (pt, inlets, pl_send, pl_recv),
        }[kind]
        target = dst.at[s] if kind == "plane" else dst.at[:, rows8(s)]
        pltpu.make_async_copy(src.at[pl.ds(0, PAIR)], target, recv.at[s]).wait()

    def low_copy(n, c):
        return out_copy(
            state.at[n, :, rows8(c)], low.at[n, :, rows8(c)], low_send.at[n, c], low_recv.at[n, c], above
        )

    def high_copy(n, c):
        return out_copy(
            state.at[n, :, rows8(c)], high.at[n, :, rows8(c)], high_send.at[n, c], high_recv.at[n, c],
            below,
        )

    def result_copy(s):
        source = state.at[4, :, rows8(s)]
        target = landed.at[pl.ds(PAIR * offset, PAIR)]
        return (
            out_copy(source, target, out_send.at[s], out_recv.at[offset], (s, home)),
            lambda: pltpu.make_async_copy(source, target, out_recv.at[offset]),
        )

    loads[0].wait()
    for load in loads[4:]:
        load.start()

    pl.semaphore_wait(barrier, 31)

    @pl.loop(0, 8)
    def _(i):
        j = (i + first_vel) % 8
        for y in range(PAIR):
            vt[PAIR * j + y] = jnp.squeeze(vel_ref[:, pl.ds(PAIR * j + y, 1), :], axis=1)
        spread_start("vel", j)
        edge_start(j)

    def column_of(row):
        count = row.shape[1]
        own = lax.broadcasted_iota(jnp.int32, (count, count), 0) == lax.broadcasted_iota(
            jnp.int32, (count, count), 1
        )
        picked = jnp.sum(jnp.where(own, jnp.broadcast_to(row, (count, count)), 0.0), axis=1, keepdims=True)
        return jnp.broadcast_to(picked, (count, 128))

    for load in loads[1:4]:
        load.wait()
    rows_ref[0] = column_of(conv_ref[...])
    rows_ref[1] = column_of(speed_ref[...])
    for part in range(8):
        pt_part = plane_ref[0, :, 128 * part : 128 * part + 128]
        for y in range(16):
            pt[y, part : part + 1, :] = pt_part[y : y + 1, :]

    row_copy = out_copy(rows_ref, row_vals.at[core], row_send, row_recv, partner)
    row_copy.start()
    row_vals[core] = rows_ref[...]

    @pl.loop(0, 8)
    def _(i):
        spread_start("plane", (i + me_s + 1) % 8)

    for load in loads[4:]:
        load.wait()
    kernel_row = jnp.dot(
        jnp.broadcast_to(filter_ref[...], (8, 512)), table_ref[...],
        precision=lax.Precision.HIGHEST, preferred_element_type=jnp.float32,
    )[0:1]
    rolled = pltpu.roll(jnp.broadcast_to(kernel_row, (256, 1024)), 0, 1, stride=1, stride_axis=0)
    b0, b1, b2, b3 = (rolled[:, 256 * i : 256 * i + 256] for i in range(4))
    for i, block in enumerate(
        (
            0.25 * ((b0 + b2) + (b1 + b3)),
            0.25 * ((b0 + b2) - (b1 + b3)),
            0.5 * (b0 - b2),
            0.5 * (b1 - b3),
        )
    ):
        weights[0, i], weights[1, i] = halves(block)
    op_parts = halves(op_ref[...])
    source_index = lax.broadcasted_iota(jnp.int32, (64, 192), 0)
    column = lax.broadcasted_iota(jnp.int32, (64, 192), 1)
    into_high = ((column % 64 == source_index) & (column < 128)).astype(jnp.bfloat16)
    into_low = ((column % 64 == source_index) & (column >= 128)).astype(jnp.bfloat16)
    op_cat[...] = (mul(op_parts[0], into_high) + mul(op_parts[1], into_low)).astype(jnp.bfloat16)
    col_ref[...] = column_of(inlet_ref[...])

    @pl.loop(0, 8)
    def _(i):
        j = (i + first_eddy) % 8
        for y in range(PAIR):
            et[PAIR * j + y] = jnp.squeeze(eddy_ref[:, pl.ds(PAIR * j + y, 1), :], axis=1)
        spread_start("eddy", j)

    @pl.loop(0, 8)
    def _(i):
        c = arrival(i)
        spread_arrived("vel", c)

        @pl.when(low_sends(0, c))
        def _():
            low_copy(0, c).start()

        @pl.when(high_sends(0, c))
        def _():
            high_copy(0, c).start()

        @pl.when(relays_in & (i == 4))
        def _():
            @pl.loop(0, 4)
            def _(k):
                arrived, onward = forward_eddy(k)
                arrived.wait()
                onward.start()

    def products(n):
        for y in range(PAIR):
            up, down = halves(state[n, y])
            dx[y] = mul(op_cat[...], jnp.concatenate([up, down, up], axis=0))
        u = state[n].reshape(128, 1024)
        v0, v1, v2, v3 = (u[:, 256 * i : 256 * i + 256] for i in range(4))
        even, odd = v0 + v2, v1 + v3

        def times(value, *which):
            up, down = halves(value)
            count = value.shape[0]
            both = jnp.concatenate([up, down], axis=0)
            found = []
            for i in which:
                wide = mul(both, weights[0, i])
                found.append(wide[:count] + wide[count:] + mul(up, weights[1, i]))
            return found

        (first,) = times(even + odd, 0)
        (second,) = times(even - odd, 1)
        straight, crossed = times(jnp.concatenate([v0 - v2, v1 - v3], axis=0), 2, 3)
        diff0 = straight[:128] - crossed[128:]
        diff1 = crossed[:128] + straight[128:]
        for i, part in enumerate(
            (
                (first + second) + diff0,
                (first - second) + diff1,
                (first + second) - diff0,
                (first - second) - diff1,
            )
        ):
            sz[:, :, 256 * i : 256 * i + 256] = part.reshape(PAIR, 64, 256)

    source_core = home % 2

    def row_value(which, y):
        row = PAIR * offset + y
        value = row_vals[source_core, which, pl.ds(row, 1), :]
        return jnp.concatenate([jnp.broadcast_to(value, (8, 128))] * 8, axis=1)

    def combine(n):
        if n == 0:
            row_copy.wait_recv()

            @pl.loop(0, 8)
            def _(s):
                spread_arrived("plane", s)

        step = (0.5 * time_step, 0.5 * time_step, time_step, 0.0)[n]
        share = time_step / 6.0 * (1.0, 2.0, 2.0, 1.0)[n]
        gusts = []
        for y in range(PAIR):
            tile = inlets[record_ref[n], y]
            gusts.append(
                jnp.concatenate(
                    [jnp.broadcast_to(tile[i : i + 1], (8, 128)) for i in range(8)], axis=1
                )
            )
        conv = [row_value(0, y) for y in range(PAIR)]
        speed = [row_value(1, y) for y in range(PAIR)]

        @pl.loop(0, 8)
        def _(i):
            c = arrival(i) if n == 0 else i
            if n == 0:
                spread_arrived("eddy", c)
            low_copy(n, c).wait_recv()
            high_copy(n, c).wait_recv()
            r = rows8(c)
            column = jnp.concatenate([col_ref[r, :]] * 8, axis=1)
            rows = [low[n, 0, r], low[n, 1, r], state[n, 0, r], state[n, 1, r], high[n, 0, r], high[n, 1, r]]
            for y in range(PAIR):
                u = rows[y + 2]
                second = (
                    16.0 * (rows[y + 1] + rows[y + 3]) - (rows[y] + rows[y + 4]) - 30.0 * u
                ) * (1.0 / 12.0)
                rate = (
                    eddy[y, r] * second
                    - (conv[y] + u) * (dx[y, r] + column * gusts[y])
                    - speed[y] * sz[y, r]
                )
                if n == 0:
                    total[y, r] = u + share * rate
                    state[1, y, r] = u + step * rate
                elif n < 3:
                    total[y, r] += share * rate
                    state[n + 1, y, r] = state[0, y, r] + step * rate
                else:
                    state[4, y, r] = total[y, r] + share * rate
            if n < 3:
                low_copy(n + 1, c).start()
                high_copy(n + 1, c).start()
            else:
                remote, local = result_copy(c)
                mine = (c == me_s) & (home == me_p)

                @pl.when(jnp.logical_not(mine))
                def _():
                    remote.start()

                @pl.when(mine)
                def _():
                    local().start()

    for n in range(4):
        products(n)
        combine(n)

    @pl.when(relays_in)
    def _():
        for k in range(4):
            forward_eddy(k)[1].wait_send()

    @pl.when(crossing)
    def _():
        edge_copy(True).wait_send()

    spread_sent("vel")
    spread_sent("plane")
    spread_sent("eddy")
    row_copy.wait_send()

    @pl.loop(0, 8)
    def _(c):
        for n in range(4):

            @pl.when(low_sends(n, c))
            def _():
                low_copy(n, c).wait_send()

            @pl.when(high_sends(n, c))
            def _():
                high_copy(n, c).wait_send()

        mine = (c == me_s) & (home == me_p)

        @pl.when(jnp.logical_not(mine))
        def _():
            result_copy(c)[0].wait_send()

        pltpu.make_async_copy(
            state.at[4, :, rows8(0)], landed.at[pl.ds(PAIR * c, PAIR)], out_recv.at[c]
        ).wait()
        for y in range(PAIR):
            out_ref[:, pl.ds(PAIR * c + y, 1), :] = jnp.expand_dims(landed[PAIR * c + y], 1)


def ring_shards(
    velocity, eddy_visc, stream_op, inlet_col, planes, record, convection, span_speed, span_filter
):
    span_len = velocity.shape[2]
    half = span_len // 2
    modes = np.arange(half)[:, None]
    angle = (modes * np.arange(span_len)[None, :] % span_len) * (2.0 * np.pi / span_len)
    table = (-2.0 / span_len * modes / half * np.sin(angle)).astype(np.float32)
    f32, dma = jnp.float32, pltpu.SemaphoreType.DMA
    result = pl.pallas_call(
        ring_kernel,
        out_shape=pltpu.VMEM((8, 16, 1024), f32),
        in_specs=[pl.BlockSpec(memory_space=pltpu.HBM)] * 10,
        out_specs=pl.BlockSpec(memory_space=pltpu.VMEM),
        scratch_shapes=[
            pltpu.VMEM((8, 16, 1024), f32),
            pltpu.VMEM((8, 16, 1024), f32),
            pltpu.VMEM((64, 64), f32),
            pltpu.VMEM((1, 64), f32),
            pltpu.VMEM((1, 16, 1024), f32),
            pltpu.SMEM((4,), jnp.int32),
            pltpu.VMEM((1, 16), f32),
            pltpu.VMEM((1, 16), f32),
            pltpu.VMEM((1, 512), f32),
            pltpu.VMEM((512, 1024), f32),
            dma((10,)),
            pltpu.VMEM((64, 128), f32),
            pltpu.VMEM((2, 16, 128), f32),
            pltpu.VMEM((16, 8, 1024), f32),
            pltpu.VMEM((16, 8, 1024), f32),
            pltpu.VMEM((16, 8, 128), f32),
            pltpu.VMEM((5, 2, 64, 1024), f32),
            pltpu.VMEM((2, 64, 1024), f32),
            pltpu.VMEM((8, 2, 8, 128), f32),
            pltpu.VMEM((2, 2, 16, 128), f32),
            pltpu.VMEM((4, 2, 64, 1024), f32),
            pltpu.VMEM((4, 2, 64, 1024), f32),
            pltpu.VMEM((2, 64, 1024), f32),
            pltpu.VMEM((2, 64, 1024), f32),
            pltpu.VMEM((2, 64, 1024), f32),
            pltpu.VMEM((2, 4, 256, 256), jnp.bfloat16),
            pltpu.VMEM((64, 192), jnp.bfloat16),
            dma((8,)), dma((8,)), dma((8,)), dma((8,)), dma((8,)), dma((8,)), dma, dma,
            dma((4, 8)), dma((4, 8)), dma((4, 8)), dma((4, 8)), dma((8,)), dma((8,)),
            pltpu.VMEM((4, 2, 8, 1024), f32), dma((4,)), dma((4,)), dma,
            pltpu.VMEM((16, 8, 1024), f32),
        ],
        compiler_params=pltpu.CompilerParams(
            collective_id=0, has_side_effects=True, vmem_limit_bytes=56 * 2**20
        ),
    )(
        velocity,
        eddy_visc,
        stream_op,
        inlet_col[None, :],
        planes,
        record,
        convection[None, :],
        span_speed[None, :],
        span_filter[None, :],
        jnp.asarray(table),
    )
    return result


def either(velocity, *others):
    fits = (
        lax.axis_size("stream") == 8
        and lax.axis_size("pitch") == 4
        and velocity.shape == (8, 16, 1024)
    )
    return (ring_shards if fits else shards)(velocity, *others)


def solution(mesh):
    placed = (
        P("stream", "pitch", None),
        P("stream", "pitch", None),
        P(),
        P(),
        P("stream", "pitch", None),
        P(),
        P("pitch"),
        P("pitch"),
        P(),
    )
    return jax.shard_map(
        either, mesh=mesh, in_specs=placed, out_specs=P("stream", "pitch", None), check_vma=False
    )
```

```python
import math

import jax
import jax.numpy as jnp
import numpy as np
from jax import lax
from jax.experimental import pallas as pl
from jax.experimental.pallas import tpu as pltpu
from jax.sharding import PartitionSpec as P

time_step = 0.25


def spread(shard, axis, root):
    mine = lax.axis_index(axis) == root
    return lax.psum(jnp.where(mine, shard, jnp.zeros_like(shard)), axis)


def with_halo(shard, sides, width):
    for axis, dim in sides:
        peers, length = (lax.axis_size(axis), shard.shape[dim])
        up = [(i, (i + 1) % peers) for i in range(peers)]
        down = [(j, i) for i, j in up]
        last = lax.slice_in_dim(shard, length - width, length, axis=dim)
        initial = lax.slice_in_dim(shard, 0, width, axis=dim)
        before = lax.ppermute(last, axis, up)
        after = lax.ppermute(initial, axis, down)
        shard = jnp.concatenate([before, shard, after], axis=dim)
    return shard


def pitch_second(padded):
    return (
        -padded[:, 0:-4]
        + 16.0 * padded[:, 1:-3]
        - 30.0 * padded[:, 2:-2]
        + 16.0 * padded[:, 3:-1]
        - padded[:, 4:]
    ) / 12.0


def shards(
    velocity, eddy_visc, stream_op, inlet_col, planes, record, convection, span_speed, span_filter
):
    cells_x, cells_y, span_len = velocity.shape
    stream_len = stream_op.shape[0]
    span_piece = span_len // lax.axis_size("stream")
    position = lax.axis_index("stream")
    half = span_len // 2
    rows_index = lax.iota(jnp.int32, span_len)[:, None]
    mode_index = lax.iota(jnp.int32, half)[None, :]
    angle = (rows_index * mode_index % span_len).astype(jnp.float32) * (2.0 * math.pi / span_len)
    table_dft = jnp.concatenate([jnp.cos(angle), jnp.sin(angle)], axis=1)
    gains = span_filter * lax.iota(jnp.float32, half) / half
    conv_rows = convection[None, :, None]
    span_rows = span_speed[None, :, None]

    def inlet_at(section):
        whole = spread(planes[0], "stream", record[section])
        return lax.dynamic_slice_in_dim(whole, position * span_piece, span_piece, 1)

    def span_part(state):
        flat = state.reshape(-1, span_len)
        coeffs = jnp.dot(
            flat, table_dft, precision=lax.Precision.HIGHEST, preferred_element_type=jnp.float32
        )
        mixed = jnp.concatenate([coeffs[:, half:] * gains, -coeffs[:, :half] * gains], axis=1)
        back = lax.dot_general(
            mixed,
            table_dft,
            (((1,), (1,)), ((), ())),
            precision=lax.Precision.HIGHEST,
            preferred_element_type=jnp.float32,
        )
        return (back * (2.0 / span_len)).reshape(state.shape)

    def section_rate(state, section):
        inlet_slice = inlet_at(section)
        pencil = lax.all_to_all(state, "stream", split_axis=2, concat_axis=0, tiled=True)
        stream_deriv = jnp.dot(
            stream_op,
            pencil.reshape(stream_len, -1),
            precision=lax.Precision.HIGHEST,
            preferred_element_type=jnp.float32,
        )
        stream_deriv = (
            stream_deriv.reshape(pencil.shape) + inlet_col[:, None, None] * inlet_slice[None, :, :]
        )
        returned = lax.all_to_all(stream_deriv, "stream", split_axis=0, concat_axis=2, tiled=True)
        padded = with_halo(state, (("pitch", 1),), 2)
        local_terms = -(conv_rows + state) * returned + eddy_visc * pitch_second(padded)
        return local_terms - span_rows * span_part(state)

    first = section_rate(velocity, 0)
    second = section_rate(velocity + 0.5 * time_step * first, 1)
    third = section_rate(velocity + 0.5 * time_step * second, 2)
    fourth = section_rate(velocity + time_step * third, 3)
    return velocity + time_step / 6.0 * (first + 2.0 * second + 2.0 * third + fourth)


CHUNK = 8
PAIR = 2
MESH_ID = pl.DeviceIdType.MESH


def place_of(rank):
    spot, turn = rank // 2, rank % 2
    plane, step = spot // 8, spot % 8
    along = step + (1 - plane) * (7 - 2 * step)
    depth = along // 2
    core = (plane + depth // 2 + step + turn + 1) % 2
    return 2 * depth + (along + 1) // 2 % 2, 2 * plane + core


def rank_of(stream, pitch):
    depth, side, plane, core = stream // 2, stream % 2, pitch // 2, pitch % 2
    along = 2 * depth + (side + depth) % 2
    step = along + (1 - plane) * (7 - 2 * along)
    return 2 * (8 * plane + step) + (core + plane + depth // 2 + step + 1) % 2


def halves(value):
    high = value.astype(jnp.bfloat16)
    return high, (value - high.astype(jnp.float32)).astype(jnp.bfloat16)


def mul(left, right):
    return jnp.dot(left, right, preferred_element_type=jnp.float32)


def ring_kernel(
    vel_hbm, eddy_hbm, op_hbm, col_hbm, plane_hbm, record_hbm, conv_hbm, speed_hbm, filter_hbm, table_hbm,
    out_ref,
    vel_ref, eddy_ref, op_ref, inlet_ref, plane_ref, record_ref, conv_ref, speed_ref, filter_ref, table_ref,
    in_sems, col_ref, rows_ref,
    vt, et, pt, state, eddy, inlets, row_vals, low, high, total, dx, sz, weights, op_cat,
    vel_send, vel_recv, eddy_send, eddy_recv, pl_send, pl_recv, row_send, row_recv,
    low_send, low_recv, high_send, high_recv, out_send, out_recv,
    eddy_via, eddy_via_recv, eddy_on, edge_send, landed,
):
    me_s, me_p = lax.axis_index("stream"), lax.axis_index("pitch")
    me = rank_of(me_s, me_p)
    home = me // 8
    offset = me % 8
    above = place_of((me + 1) % 32)
    below = place_of((me + 31) % 32)
    partner = (me_s, me_p + 1 - 2 * (me_p % 2))
    core = me_p % 2
    upper = me_s // 4
    group_upper = 1 - (me_p + 1) // 2 % 2
    feeds = (me_s == 2) | (me_s == 4)
    relays = (me_s == 3) | (me_s == 5)
    feeds_in = feeds & (group_upper != upper)
    relays_in = relays & (group_upper == upper)
    crossing = group_upper != upper
    mirrored = (me_s + 2 * (1 - upper)) % 4
    first_vel = jnp.where(crossing & (mirrored < 2), 6, 2)
    first_eddy = jnp.where(crossing & (mirrored == 1), 6, 2)
    edge = 7 * (1 - core)
    edge_peer = place_of((8 * me_p + edge + 33 - 2 * core) % 32)
    ends_low, ends_high = me % 16 == 7, me % 16 == 8
    inner = (offset >= 2) & (offset <= 5)

    def arrival(i):
        turn = jnp.where(inner, 7 - i % 4, 4 + i % 4)
        return jnp.where(i < 4, 4 * upper + i % 4, jnp.where(upper == 1, (turn + 2) % 4, turn))

    loads = [
        pltpu.make_async_copy(source, target, in_sems.at[i])
        for i, (source, target) in enumerate(
            (
                (vel_hbm, vel_ref), (plane_hbm, plane_ref), (conv_hbm, conv_ref), (speed_hbm, speed_ref),
                (eddy_hbm, eddy_ref), (filter_hbm, filter_ref), (table_hbm, table_ref), (op_hbm, op_ref),
                (col_hbm, inlet_ref), (record_hbm, record_ref),
            )
        )
    ]
    for load in loads[:4]:
        load.start()

    barrier = pltpu.get_barrier_semaphore()

    @pl.loop(1, 32)
    def _(step):
        other = (me_s * 4 + me_p + step) % 32
        pl.semaphore_signal(barrier, inc=1, device_id=(other // 4, other % 4), device_id_type=MESH_ID)

    def rows8(index):
        return pl.ds(pl.multiple_of(index * CHUNK, CHUNK), CHUNK)

    def out_copy(src, dst, send, recv, device):
        return pltpu.make_async_remote_copy(
            src_ref=src, dst_ref=dst, send_sem=send, recv_sem=recv, device_id=device,
            device_id_type=MESH_ID,
        )

    def spread_copy(kind, j):
        src, dst, send, recv = {
            "vel": (vt, state.at[0], vel_send, vel_recv),
            "eddy": (et, eddy, eddy_send, eddy_recv),
            "plane": (pt, inlets, pl_send, pl_recv),
        }[kind]
        source = src.at[pl.ds(PAIR * j, PAIR)]
        target = dst.at[me_s] if kind == "plane" else dst.at[:, rows8(me_s)]
        rank = 8 * me_p + j
        return (
            rank,
            out_copy(source, target, send.at[j], recv.at[me_s], place_of(rank)),
            lambda: pltpu.make_async_copy(source, target, recv.at[me_s]),
        )

    def spread_start(kind, j):
        rank, remote, local = spread_copy(kind, j)

        via = feeds_in & (j >= 2) & (j <= 5) if kind == "eddy" else False

        @pl.when((rank != me) & jnp.logical_not(via))
        def _():
            remote.start()

        @pl.when(rank == me)
        def _():
            local().start()

        if kind == "eddy":

            @pl.when(via)
            def _():
                k = (j + 6) % 8
                out_copy(
                    et.at[pl.ds(PAIR * j, PAIR)], eddy_via.at[k], eddy_send.at[j], eddy_via_recv.at[k],
                    (me_s + 1, me_p + 1 - 2 * core),
                ).start()

    def forward_eddy(k):
        source = (me_s + 7) % 8
        return (
            pltpu.make_async_copy(eddy_via.at[k], eddy_via.at[k], eddy_via_recv.at[k]),
            out_copy(
                eddy_via.at[k], eddy.at[:, rows8(source)], eddy_on.at[k], eddy_recv.at[source],
                place_of(8 * (me_p + 1 - 2 * core) + 2 + k),
            ),
        )

    def edge_copy(to_low):
        dst, recv = (low, low_recv) if to_low else (high, high_recv)
        return out_copy(
            vt.at[pl.ds(PAIR * edge, PAIR)], dst.at[0, :, rows8(me_s)], edge_send, recv.at[0, me_s],
            edge_peer,
        )

    def edge_start(j):
        @pl.when(crossing & (j == edge) & (core == 0))
        def _():
            edge_copy(True).start()

        @pl.when(crossing & (j == edge) & (core == 1))
        def _():
            edge_copy(False).start()

    def low_sends(n, c):
        return jnp.logical_not(ends_low & (c // 4 != upper)) if n == 0 else True

    def high_sends(n, c):
        return jnp.logical_not(ends_high & (c // 4 != upper)) if n == 0 else True

    def spread_sent(kind):
        @pl.loop(0, 8)
        def _(j):
            rank, remote, _local = spread_copy(kind, j)

            @pl.when(rank != me)
            def _():
                remote.wait_send()

    def spread_arrived(kind, s):
        src, dst, send, recv = {
            "vel": (vt, state.at[0], vel_send, vel_recv),
            "eddy": (et, eddy, eddy_send, eddy_recv),
            "plane": (pt, inlets, pl_send, pl_recv),
        }[kind]
        target = dst.at[s] if kind == "plane" else dst.at[:, rows8(s)]
        pltpu.make_async_copy(src.at[pl.ds(0, PAIR)], target, recv.at[s]).wait()

    def low_copy(n, c):
        return out_copy(
            state.at[n, :, rows8(c)], low.at[n, :, rows8(c)], low_send.at[n, c], low_recv.at[n, c], above
        )

    def high_copy(n, c):
        return out_copy(
            state.at[n, :, rows8(c)], high.at[n, :, rows8(c)], high_send.at[n, c], high_recv.at[n, c],
            below,
        )

    def result_copy(s):
        source = state.at[4, :, rows8(s)]
        target = landed.at[pl.ds(PAIR * offset, PAIR)]
        return (
            out_copy(source, target, out_send.at[s], out_recv.at[offset], (s, home)),
            lambda: pltpu.make_async_copy(source, target, out_recv.at[offset]),
        )

    loads[0].wait()
    for load in loads[4:]:
        load.start()

    pl.semaphore_wait(barrier, 31)

    @pl.loop(0, 8)
    def _(i):
        j = (i + first_vel) % 8
        for y in range(PAIR):
            vt[PAIR * j + y] = jnp.squeeze(vel_ref[:, pl.ds(PAIR * j + y, 1), :], axis=1)
        spread_start("vel", j)
        edge_start(j)

    def column_of(row):
        count = row.shape[1]
        own = lax.broadcasted_iota(jnp.int32, (count, count), 0) == lax.broadcasted_iota(
            jnp.int32, (count, count), 1
        )
        picked = jnp.sum(jnp.where(own, jnp.broadcast_to(row, (count, count)), 0.0), axis=1, keepdims=True)
        return jnp.broadcast_to(picked, (count, 128))

    for load in loads[1:4]:
        load.wait()
    rows_ref[0] = column_of(conv_ref[...])
    rows_ref[1] = column_of(speed_ref[...])
    for part in range(8):
        pt_part = plane_ref[0, :, 128 * part : 128 * part + 128]
        for y in range(16):
            pt[y, part : part + 1, :] = pt_part[y : y + 1, :]

    row_copy = out_copy(rows_ref, row_vals.at[core], row_send, row_recv, partner)
    row_copy.start()
    row_vals[core] = rows_ref[...]

    @pl.loop(0, 8)
    def _(i):
        spread_start("plane", (i + me_s + 1) % 8)

    for load in loads[4:]:
        load.wait()
    kernel_row = jnp.dot(
        jnp.broadcast_to(filter_ref[...], (8, 512)), table_ref[...],
        precision=lax.Precision.HIGHEST, preferred_element_type=jnp.float32,
    )[0:1]
    rolled = pltpu.roll(jnp.broadcast_to(kernel_row, (256, 1024)), 0, 1, stride=1, stride_axis=0)
    b0, b1, b2, b3 = (rolled[:, 256 * i : 256 * i + 256] for i in range(4))
    for i, block in enumerate(
        (
            0.25 * ((b0 + b2) + (b1 + b3)),
            0.25 * ((b0 + b2) - (b1 + b3)),
            0.5 * (b0 - b2),
            0.5 * (b1 - b3),
        )
    ):
        weights[0, i], weights[1, i] = halves(block)
    op_parts = halves(op_ref[...])
    source_index = lax.broadcasted_iota(jnp.int32, (64, 192), 0)
    column = lax.broadcasted_iota(jnp.int32, (64, 192), 1)
    into_high = ((column % 64 == source_index) & (column < 128)).astype(jnp.bfloat16)
    into_low = ((column % 64 == source_index) & (column >= 128)).astype(jnp.bfloat16)
    op_cat[...] = (mul(op_parts[0], into_high) + mul(op_parts[1], into_low)).astype(jnp.bfloat16)
    col_ref[...] = column_of(inlet_ref[...])

    @pl.loop(0, 8)
    def _(i):
        j = (i + first_eddy) % 8
        for y in range(PAIR):
            et[PAIR * j + y] = jnp.squeeze(eddy_ref[:, pl.ds(PAIR * j + y, 1), :], axis=1)
        spread_start("eddy", j)

    @pl.loop(0, 8)
    def _(i):
        c = arrival(i)
        spread_arrived("vel", c)

        @pl.when(low_sends(0, c))
        def _():
            low_copy(0, c).start()

        @pl.when(high_sends(0, c))
        def _():
            high_copy(0, c).start()

        @pl.when(relays_in & (i == 2))
        def _():
            @pl.loop(0, 4)
            def _(k):
                arrived, onward = forward_eddy(k)
                arrived.wait()
                onward.start()

    def products(n):
        for y in range(PAIR):
            up, down = halves(state[n, y])
            dx[y] = mul(op_cat[...], jnp.concatenate([up, down, up], axis=0))
        u = state[n].reshape(128, 1024)
        v0, v1, v2, v3 = (u[:, 256 * i : 256 * i + 256] for i in range(4))
        even, odd = v0 + v2, v1 + v3

        def times(value, *which):
            up, down = halves(value)
            count = value.shape[0]
            both = jnp.concatenate([up, down], axis=0)
            found = []
            for i in which:
                wide = mul(both, weights[0, i])
                found.append(wide[:count] + wide[count:] + mul(up, weights[1, i]))
            return found

        (first,) = times(even + odd, 0)
        (second,) = times(even - odd, 1)
        straight, crossed = times(jnp.concatenate([v0 - v2, v1 - v3], axis=0), 2, 3)
        diff0 = straight[:128] - crossed[128:]
        diff1 = crossed[:128] + straight[128:]
        for i, part in enumerate(
            (
                (first + second) + diff0,
                (first - second) + diff1,
                (first + second) - diff0,
                (first - second) - diff1,
            )
        ):
            sz[:, :, 256 * i : 256 * i + 256] = part.reshape(PAIR, 64, 256)

    source_core = home % 2

    def row_value(which, y):
        row = PAIR * offset + y
        value = row_vals[source_core, which, pl.ds(row, 1), :]
        return jnp.concatenate([jnp.broadcast_to(value, (8, 128))] * 8, axis=1)

    def combine(n):
        if n == 0:
            row_copy.wait_recv()

            @pl.loop(0, 8)
            def _(s):
                spread_arrived("plane", s)

        step = (0.5 * time_step, 0.5 * time_step, time_step, 0.0)[n]
        share = time_step / 6.0 * (1.0, 2.0, 2.0, 1.0)[n]
        gusts = []
        for y in range(PAIR):
            tile = inlets[record_ref[n], y]
            gusts.append(
                jnp.concatenate(
                    [jnp.broadcast_to(tile[i : i + 1], (8, 128)) for i in range(8)], axis=1
                )
            )
        conv = [row_value(0, y) for y in range(PAIR)]
        speed = [row_value(1, y) for y in range(PAIR)]

        @pl.loop(0, 8)
        def _(i):
            c = arrival(i) if n == 0 else i
            if n == 0:
                spread_arrived("eddy", c)
            low_copy(n, c).wait_recv()
            high_copy(n, c).wait_recv()
            r = rows8(c)
            column = jnp.concatenate([col_ref[r, :]] * 8, axis=1)
            rows = [low[n, 0, r], low[n, 1, r], state[n, 0, r], state[n, 1, r], high[n, 0, r], high[n, 1, r]]
            for y in range(PAIR):
                u = rows[y + 2]
                second = (
                    16.0 * (rows[y + 1] + rows[y + 3]) - (rows[y] + rows[y + 4]) - 30.0 * u
                ) * (1.0 / 12.0)
                rate = (
                    eddy[y, r] * second
                    - (conv[y] + u) * (dx[y, r] + column * gusts[y])
                    - speed[y] * sz[y, r]
                )
                if n == 0:
                    total[y, r] = u + share * rate
                    state[1, y, r] = u + step * rate
                elif n < 3:
                    total[y, r] += share * rate
                    state[n + 1, y, r] = state[0, y, r] + step * rate
                else:
                    state[4, y, r] = total[y, r] + share * rate
            if n < 3:
                low_copy(n + 1, c).start()
                high_copy(n + 1, c).start()
            else:
                remote, local = result_copy(c)
                mine = (c == me_s) & (home == me_p)

                @pl.when(jnp.logical_not(mine))
                def _():
                    remote.start()

                @pl.when(mine)
                def _():
                    local().start()

    for n in range(4):
        products(n)
        combine(n)

    @pl.when(relays_in)
    def _():
        for k in range(4):
            forward_eddy(k)[1].wait_send()

    @pl.when(crossing)
    def _():
        edge_copy(True).wait_send()

    spread_sent("vel")
    spread_sent("plane")
    spread_sent("eddy")
    row_copy.wait_send()

    @pl.loop(0, 8)
    def _(c):
        for n in range(4):

            @pl.when(low_sends(n, c))
            def _():
                low_copy(n, c).wait_send()

            @pl.when(high_sends(n, c))
            def _():
                high_copy(n, c).wait_send()

        mine = (c == me_s) & (home == me_p)

        @pl.when(jnp.logical_not(mine))
        def _():
            result_copy(c)[0].wait_send()

        pltpu.make_async_copy(
            state.at[4, :, rows8(0)], landed.at[pl.ds(PAIR * c, PAIR)], out_recv.at[c]
        ).wait()
        for y in range(PAIR):
            out_ref[:, pl.ds(PAIR * c + y, 1), :] = jnp.expand_dims(landed[PAIR * c + y], 1)


def ring_shards(
    velocity, eddy_visc, stream_op, inlet_col, planes, record, convection, span_speed, span_filter
):
    span_len = velocity.shape[2]
    half = span_len // 2
    modes = np.arange(half)[:, None]
    angle = (modes * np.arange(span_len)[None, :] % span_len) * (2.0 * np.pi / span_len)
    table = (-2.0 / span_len * modes / half * np.sin(angle)).astype(np.float32)
    f32, dma = jnp.float32, pltpu.SemaphoreType.DMA
    result = pl.pallas_call(
        ring_kernel,
        out_shape=pltpu.VMEM((8, 16, 1024), f32),
        in_specs=[pl.BlockSpec(memory_space=pltpu.HBM)] * 10,
        out_specs=pl.BlockSpec(memory_space=pltpu.VMEM),
        scratch_shapes=[
            pltpu.VMEM((8, 16, 1024), f32),
            pltpu.VMEM((8, 16, 1024), f32),
            pltpu.VMEM((64, 64), f32),
            pltpu.VMEM((1, 64), f32),
            pltpu.VMEM((1, 16, 1024), f32),
            pltpu.SMEM((4,), jnp.int32),
            pltpu.VMEM((1, 16), f32),
            pltpu.VMEM((1, 16), f32),
            pltpu.VMEM((1, 512), f32),
            pltpu.VMEM((512, 1024), f32),
            dma((10,)),
            pltpu.VMEM((64, 128), f32),
            pltpu.VMEM((2, 16, 128), f32),
            pltpu.VMEM((16, 8, 1024), f32),
            pltpu.VMEM((16, 8, 1024), f32),
            pltpu.VMEM((16, 8, 128), f32),
            pltpu.VMEM((5, 2, 64, 1024), f32),
            pltpu.VMEM((2, 64, 1024), f32),
            pltpu.VMEM((8, 2, 8, 128), f32),
            pltpu.VMEM((2, 2, 16, 128), f32),
            pltpu.VMEM((4, 2, 64, 1024), f32),
            pltpu.VMEM((4, 2, 64, 1024), f32),
            pltpu.VMEM((2, 64, 1024), f32),
            pltpu.VMEM((2, 64, 1024), f32),
            pltpu.VMEM((2, 64, 1024), f32),
            pltpu.VMEM((2, 4, 256, 256), jnp.bfloat16),
            pltpu.VMEM((64, 192), jnp.bfloat16),
            dma((8,)), dma((8,)), dma((8,)), dma((8,)), dma((8,)), dma((8,)), dma, dma,
            dma((4, 8)), dma((4, 8)), dma((4, 8)), dma((4, 8)), dma((8,)), dma((8,)),
            pltpu.VMEM((4, 2, 8, 1024), f32), dma((4,)), dma((4,)), dma,
            pltpu.VMEM((16, 8, 1024), f32),
        ],
        compiler_params=pltpu.CompilerParams(
            collective_id=0, has_side_effects=True, vmem_limit_bytes=56 * 2**20
        ),
    )(
        velocity,
        eddy_visc,
        stream_op,
        inlet_col[None, :],
        planes,
        record,
        convection[None, :],
        span_speed[None, :],
        span_filter[None, :],
        jnp.asarray(table),
    )
    return result


def either(velocity, *others):
    fits = (
        lax.axis_size("stream") == 8
        and lax.axis_size("pitch") == 4
        and velocity.shape == (8, 16, 1024)
    )
    return (ring_shards if fits else shards)(velocity, *others)


def solution(mesh):
    placed = (
        P("stream", "pitch", None),
        P("stream", "pitch", None),
        P(),
        P(),
        P("stream", "pitch", None),
        P(),
        P("pitch"),
        P("pitch"),
        P(),
    )
    return jax.shard_map(
        either, mesh=mesh, in_specs=placed, out_specs=P("stream", "pitch", None), check_vma=False
    )
```

```python
import math

import jax
import jax.numpy as jnp
import numpy as np
from jax import lax
from jax.experimental import pallas as pl
from jax.experimental.pallas import tpu as pltpu
from jax.sharding import PartitionSpec as P

time_step = 0.25


def spread(shard, axis, root):
    mine = lax.axis_index(axis) == root
    return lax.psum(jnp.where(mine, shard, jnp.zeros_like(shard)), axis)


def with_halo(shard, sides, width):
    for axis, dim in sides:
        peers, length = (lax.axis_size(axis), shard.shape[dim])
        up = [(i, (i + 1) % peers) for i in range(peers)]
        down = [(j, i) for i, j in up]
        last = lax.slice_in_dim(shard, length - width, length, axis=dim)
        initial = lax.slice_in_dim(shard, 0, width, axis=dim)
        before = lax.ppermute(last, axis, up)
        after = lax.ppermute(initial, axis, down)
        shard = jnp.concatenate([before, shard, after], axis=dim)
    return shard


def pitch_second(padded):
    return (
        -padded[:, 0:-4]
        + 16.0 * padded[:, 1:-3]
        - 30.0 * padded[:, 2:-2]
        + 16.0 * padded[:, 3:-1]
        - padded[:, 4:]
    ) / 12.0


def shards(
    velocity, eddy_visc, stream_op, inlet_col, planes, record, convection, span_speed, span_filter
):
    cells_x, cells_y, span_len = velocity.shape
    stream_len = stream_op.shape[0]
    span_piece = span_len // lax.axis_size("stream")
    position = lax.axis_index("stream")
    half = span_len // 2
    rows_index = lax.iota(jnp.int32, span_len)[:, None]
    mode_index = lax.iota(jnp.int32, half)[None, :]
    angle = (rows_index * mode_index % span_len).astype(jnp.float32) * (2.0 * math.pi / span_len)
    table_dft = jnp.concatenate([jnp.cos(angle), jnp.sin(angle)], axis=1)
    gains = span_filter * lax.iota(jnp.float32, half) / half
    conv_rows = convection[None, :, None]
    span_rows = span_speed[None, :, None]

    def inlet_at(section):
        whole = spread(planes[0], "stream", record[section])
        return lax.dynamic_slice_in_dim(whole, position * span_piece, span_piece, 1)

    def span_part(state):
        flat = state.reshape(-1, span_len)
        coeffs = jnp.dot(
            flat, table_dft, precision=lax.Precision.HIGHEST, preferred_element_type=jnp.float32
        )
        mixed = jnp.concatenate([coeffs[:, half:] * gains, -coeffs[:, :half] * gains], axis=1)
        back = lax.dot_general(
            mixed,
            table_dft,
            (((1,), (1,)), ((), ())),
            precision=lax.Precision.HIGHEST,
            preferred_element_type=jnp.float32,
        )
        return (back * (2.0 / span_len)).reshape(state.shape)

    def section_rate(state, section):
        inlet_slice = inlet_at(section)
        pencil = lax.all_to_all(state, "stream", split_axis=2, concat_axis=0, tiled=True)
        stream_deriv = jnp.dot(
            stream_op,
            pencil.reshape(stream_len, -1),
            precision=lax.Precision.HIGHEST,
            preferred_element_type=jnp.float32,
        )
        stream_deriv = (
            stream_deriv.reshape(pencil.shape) + inlet_col[:, None, None] * inlet_slice[None, :, :]
        )
        returned = lax.all_to_all(stream_deriv, "stream", split_axis=0, concat_axis=2, tiled=True)
        padded = with_halo(state, (("pitch", 1),), 2)
        local_terms = -(conv_rows + state) * returned + eddy_visc * pitch_second(padded)
        return local_terms - span_rows * span_part(state)

    first = section_rate(velocity, 0)
    second = section_rate(velocity + 0.5 * time_step * first, 1)
    third = section_rate(velocity + 0.5 * time_step * second, 2)
    fourth = section_rate(velocity + time_step * third, 3)
    return velocity + time_step / 6.0 * (first + 2.0 * second + 2.0 * third + fourth)


CHUNK = 8
PAIR = 2
MESH_ID = pl.DeviceIdType.MESH


def place_of(rank):
    spot, turn = rank // 2, rank % 2
    plane, step = spot // 8, spot % 8
    along = step + (1 - plane) * (7 - 2 * step)
    depth = along // 2
    core = (plane + depth // 2 + step + turn + 1) % 2
    return 2 * depth + (along + 1) // 2 % 2, 2 * plane + core


def rank_of(stream, pitch):
    depth, side, plane, core = stream // 2, stream % 2, pitch // 2, pitch % 2
    along = 2 * depth + (side + depth) % 2
    step = along + (1 - plane) * (7 - 2 * along)
    return 2 * (8 * plane + step) + (core + plane + depth // 2 + step + 1) % 2


def halves(value):
    high = value.astype(jnp.bfloat16)
    return high, (value - high.astype(jnp.float32)).astype(jnp.bfloat16)


def mul(left, right):
    return jnp.dot(left, right, preferred_element_type=jnp.float32)


def ring_kernel(
    vel_hbm, eddy_hbm, op_hbm, col_hbm, plane_hbm, record_hbm, conv_hbm, speed_hbm, filter_hbm, table_hbm,
    out_ref,
    vel_ref, eddy_ref, op_ref, inlet_ref, plane_ref, record_ref, conv_ref, speed_ref, filter_ref, table_ref,
    in_sems, col_ref, rows_ref,
    vt, et, pt, state, eddy, inlets, row_vals, low, high, total, dx, sz, weights, op_cat,
    vel_send, vel_recv, eddy_send, eddy_recv, pl_send, pl_recv, row_send, row_recv,
    low_send, low_recv, high_send, high_recv, out_send, out_recv,
    eddy_via, eddy_via_recv, eddy_on, edge_send, landed,
):
    me_s, me_p = lax.axis_index("stream"), lax.axis_index("pitch")
    me = rank_of(me_s, me_p)
    home = me // 8
    offset = me % 8
    above = place_of((me + 1) % 32)
    below = place_of((me + 31) % 32)
    partner = (me_s, me_p + 1 - 2 * (me_p % 2))
    core = me_p % 2
    upper = me_s // 4
    group_upper = 1 - (me_p + 1) // 2 % 2
    feeds = (me_s == 2) | (me_s == 4)
    relays = (me_s == 3) | (me_s == 5)
    feeds_in = feeds & (group_upper != upper)
    relays_in = relays & (group_upper == upper)
    crossing = group_upper != upper
    mirrored = (me_s + 2 * (1 - upper)) % 4
    first_vel = jnp.where(crossing & (mirrored < 2), 6, 2)
    first_eddy = jnp.where(crossing & (mirrored == 1), 6, 2)
    edge = 7 * (1 - core)
    edge_peer = place_of((8 * me_p + edge + 33 - 2 * core) % 32)
    ends_low, ends_high = me % 16 == 7, me % 16 == 8
    inner = (offset >= 2) & (offset <= 5)

    def arrival(i):
        turn = jnp.where(inner, 7 - i % 4, 4 + i % 4)
        return jnp.where(i < 4, 4 * upper + i % 4, jnp.where(upper == 1, (turn + 2) % 4, turn))

    loads = [
        pltpu.make_async_copy(source, target, in_sems.at[i])
        for i, (source, target) in enumerate(
            (
                (vel_hbm, vel_ref), (plane_hbm, plane_ref), (conv_hbm, conv_ref), (speed_hbm, speed_ref),
                (eddy_hbm, eddy_ref), (filter_hbm, filter_ref), (table_hbm, table_ref), (op_hbm, op_ref),
                (col_hbm, inlet_ref), (record_hbm, record_ref),
            )
        )
    ]
    barrier = pltpu.get_barrier_semaphore()
    loads[0].start()

    @pl.loop(1, 32)
    def _(step):
        other = (me_s * 4 + me_p + 32 - step) % 32
        pl.semaphore_signal(barrier, inc=1, device_id=(other // 4, other % 4), device_id_type=MESH_ID)

    for load in loads[1:4]:
        load.start()

    def rows8(index):
        return pl.ds(pl.multiple_of(index * CHUNK, CHUNK), CHUNK)

    def out_copy(src, dst, send, recv, device):
        return pltpu.make_async_remote_copy(
            src_ref=src, dst_ref=dst, send_sem=send, recv_sem=recv, device_id=device,
            device_id_type=MESH_ID,
        )

    def spread_copy(kind, j):
        src, dst, send, recv = {
            "vel": (vt, state.at[0], vel_send, vel_recv),
            "eddy": (et, eddy, eddy_send, eddy_recv),
            "plane": (pt, inlets, pl_send, pl_recv),
        }[kind]
        source = src.at[pl.ds(PAIR * j, PAIR)]
        target = dst.at[me_s] if kind == "plane" else dst.at[:, rows8(me_s)]
        rank = 8 * me_p + j
        return (
            rank,
            out_copy(source, target, send.at[j], recv.at[me_s], place_of(rank)),
            lambda: pltpu.make_async_copy(source, target, recv.at[me_s]),
        )

    def spread_start(kind, j):
        rank, remote, local = spread_copy(kind, j)

        via = feeds_in & (j >= 2) & (j <= 5) if kind == "eddy" else False

        @pl.when((rank != me) & jnp.logical_not(via))
        def _():
            remote.start()

        @pl.when(rank == me)
        def _():
            local().start()

        if kind == "eddy":

            @pl.when(via)
            def _():
                k = (j + 6) % 8
                out_copy(
                    et.at[pl.ds(PAIR * j, PAIR)], eddy_via.at[k], eddy_send.at[j], eddy_via_recv.at[k],
                    (me_s + 1, me_p + 1 - 2 * core),
                ).start()

    def forward_eddy(k):
        source = (me_s + 7) % 8
        return (
            pltpu.make_async_copy(eddy_via.at[k], eddy_via.at[k], eddy_via_recv.at[k]),
            out_copy(
                eddy_via.at[k], eddy.at[:, rows8(source)], eddy_on.at[k], eddy_recv.at[source],
                place_of(8 * (me_p + 1 - 2 * core) + 2 + k),
            ),
        )

    def edge_copy(to_low):
        dst, recv = (low, low_recv) if to_low else (high, high_recv)
        return out_copy(
            vt.at[pl.ds(PAIR * edge, PAIR)], dst.at[0, :, rows8(me_s)], edge_send, recv.at[0, me_s],
            edge_peer,
        )

    def edge_start(j):
        @pl.when(crossing & (j == edge) & (core == 0))
        def _():
            edge_copy(True).start()

        @pl.when(crossing & (j == edge) & (core == 1))
        def _():
            edge_copy(False).start()

    def low_sends(n, c):
        return jnp.logical_not(ends_low & (c // 4 != upper)) if n == 0 else True

    def high_sends(n, c):
        return jnp.logical_not(ends_high & (c // 4 != upper)) if n == 0 else True

    def spread_sent(kind):
        @pl.loop(0, 8)
        def _(j):
            rank, remote, _local = spread_copy(kind, j)

            @pl.when(rank != me)
            def _():
                remote.wait_send()

    def spread_arrived(kind, s):
        src, dst, send, recv = {
            "vel": (vt, state.at[0], vel_send, vel_recv),
            "eddy": (et, eddy, eddy_send, eddy_recv),
            "plane": (pt, inlets, pl_send, pl_recv),
        }[kind]
        target = dst.at[s] if kind == "plane" else dst.at[:, rows8(s)]
        pltpu.make_async_copy(src.at[pl.ds(0, PAIR)], target, recv.at[s]).wait()

    def low_copy(n, c):
        return out_copy(
            state.at[n, :, rows8(c)], low.at[n, :, rows8(c)], low_send.at[n, c], low_recv.at[n, c], above
        )

    def high_copy(n, c):
        return out_copy(
            state.at[n, :, rows8(c)], high.at[n, :, rows8(c)], high_send.at[n, c], high_recv.at[n, c],
            below,
        )

    def result_copy(s):
        source = state.at[4, :, rows8(s)]
        target = landed.at[pl.ds(PAIR * offset, PAIR)]
        return (
            out_copy(source, target, out_send.at[s], out_recv.at[offset], (s, home)),
            lambda: pltpu.make_async_copy(source, target, out_recv.at[offset]),
        )

    loads[0].wait()
    for load in loads[4:]:
        load.start()

    pl.semaphore_wait(barrier, 31)

    @pl.loop(0, 8)
    def _(i):
        j = (i + first_vel) % 8
        for y in range(PAIR):
            vt[PAIR * j + y] = jnp.squeeze(vel_ref[:, pl.ds(PAIR * j + y, 1), :], axis=1)
        spread_start("vel", j)
        edge_start(j)

    def column_of(row):
        count = row.shape[1]
        own = lax.broadcasted_iota(jnp.int32, (count, count), 0) == lax.broadcasted_iota(
            jnp.int32, (count, count), 1
        )
        picked = jnp.sum(jnp.where(own, jnp.broadcast_to(row, (count, count)), 0.0), axis=1, keepdims=True)
        return jnp.broadcast_to(picked, (count, 128))

    for load in loads[1:4]:
        load.wait()
    rows_ref[0] = column_of(conv_ref[...])
    rows_ref[1] = column_of(speed_ref[...])
    for part in range(8):
        pt_part = plane_ref[0, :, 128 * part : 128 * part + 128]
        for y in range(16):
            pt[y, part : part + 1, :] = pt_part[y : y + 1, :]

    row_copy = out_copy(rows_ref, row_vals.at[core], row_send, row_recv, partner)
    row_copy.start()
    row_vals[core] = rows_ref[...]

    @pl.loop(0, 8)
    def _(i):
        spread_start("plane", (i + me_s + 1) % 8)

    for load in loads[4:]:
        load.wait()
    kernel_row = jnp.dot(
        jnp.broadcast_to(filter_ref[...], (8, 512)), table_ref[...],
        precision=lax.Precision.HIGHEST, preferred_element_type=jnp.float32,
    )[0:1]
    rolled = pltpu.roll(jnp.broadcast_to(kernel_row, (256, 1024)), 0, 1, stride=1, stride_axis=0)
    b0, b1, b2, b3 = (rolled[:, 256 * i : 256 * i + 256] for i in range(4))
    for i, block in enumerate(
        (
            0.25 * ((b0 + b2) + (b1 + b3)),
            0.25 * ((b0 + b2) - (b1 + b3)),
            0.5 * (b0 - b2),
            0.5 * (b1 - b3),
        )
    ):
        weights[0, i], weights[1, i] = halves(block)
    op_parts = halves(op_ref[...])
    source_index = lax.broadcasted_iota(jnp.int32, (64, 192), 0)
    column = lax.broadcasted_iota(jnp.int32, (64, 192), 1)
    into_high = ((column % 64 == source_index) & (column < 128)).astype(jnp.bfloat16)
    into_low = ((column % 64 == source_index) & (column >= 128)).astype(jnp.bfloat16)
    op_cat[...] = (mul(op_parts[0], into_high) + mul(op_parts[1], into_low)).astype(jnp.bfloat16)
    col_ref[...] = column_of(inlet_ref[...])

    @pl.loop(0, 8)
    def _(i):
        j = (i + first_eddy) % 8
        for y in range(PAIR):
            et[PAIR * j + y] = jnp.squeeze(eddy_ref[:, pl.ds(PAIR * j + y, 1), :], axis=1)
        spread_start("eddy", j)

    @pl.loop(0, 8)
    def _(i):
        c = arrival(i)
        spread_arrived("vel", c)

        @pl.when(low_sends(0, c))
        def _():
            low_copy(0, c).start()

        @pl.when(high_sends(0, c))
        def _():
            high_copy(0, c).start()

        @pl.when(relays_in & (i == 4))
        def _():
            @pl.loop(0, 4)
            def _(k):
                arrived, onward = forward_eddy(k)
                arrived.wait()
                onward.start()

    def products(n):
        for y in range(PAIR):
            up, down = halves(state[n, y])
            dx[y] = mul(op_cat[...], jnp.concatenate([up, down, up], axis=0))
        u = state[n].reshape(128, 1024)
        v0, v1, v2, v3 = (u[:, 256 * i : 256 * i + 256] for i in range(4))
        even, odd = v0 + v2, v1 + v3

        def times(value, *which):
            up, down = halves(value)
            count = value.shape[0]
            both = jnp.concatenate([up, down], axis=0)
            found = []
            for i in which:
                wide = mul(both, weights[0, i])
                found.append(wide[:count] + wide[count:] + mul(up, weights[1, i]))
            return found

        (first,) = times(even + odd, 0)
        (second,) = times(even - odd, 1)
        straight, crossed = times(jnp.concatenate([v0 - v2, v1 - v3], axis=0), 2, 3)
        diff0 = straight[:128] - crossed[128:]
        diff1 = crossed[:128] + straight[128:]
        for i, part in enumerate(
            (
                (first + second) + diff0,
                (first - second) + diff1,
                (first + second) - diff0,
                (first - second) - diff1,
            )
        ):
            sz[:, :, 256 * i : 256 * i + 256] = part.reshape(PAIR, 64, 256)

    source_core = home % 2

    def row_value(which, y):
        row = PAIR * offset + y
        value = row_vals[source_core, which, pl.ds(row, 1), :]
        return jnp.concatenate([jnp.broadcast_to(value, (8, 128))] * 8, axis=1)

    def combine(n):
        if n == 0:
            row_copy.wait_recv()

            @pl.loop(0, 8)
            def _(s):
                spread_arrived("plane", s)

        step = (0.5 * time_step, 0.5 * time_step, time_step, 0.0)[n]
        share = time_step / 6.0 * (1.0, 2.0, 2.0, 1.0)[n]
        gusts = []
        for y in range(PAIR):
            tile = inlets[record_ref[n], y]
            gusts.append(
                jnp.concatenate(
                    [jnp.broadcast_to(tile[i : i + 1], (8, 128)) for i in range(8)], axis=1
                )
            )
        conv = [row_value(0, y) for y in range(PAIR)]
        speed = [row_value(1, y) for y in range(PAIR)]

        @pl.loop(0, 8)
        def _(i):
            c = arrival(i) if n == 0 else i
            if n == 0:
                spread_arrived("eddy", c)
            low_copy(n, c).wait_recv()
            high_copy(n, c).wait_recv()
            r = rows8(c)
            column = jnp.concatenate([col_ref[r, :]] * 8, axis=1)
            rows = [low[n, 0, r], low[n, 1, r], state[n, 0, r], state[n, 1, r], high[n, 0, r], high[n, 1, r]]
            for y in range(PAIR):
                u = rows[y + 2]
                second = (
                    16.0 * (rows[y + 1] + rows[y + 3]) - (rows[y] + rows[y + 4]) - 30.0 * u
                ) * (1.0 / 12.0)
                rate = (
                    eddy[y, r] * second
                    - (conv[y] + u) * (dx[y, r] + column * gusts[y])
                    - speed[y] * sz[y, r]
                )
                if n == 0:
                    total[y, r] = u + share * rate
                    state[1, y, r] = u + step * rate
                elif n < 3:
                    total[y, r] += share * rate
                    state[n + 1, y, r] = state[0, y, r] + step * rate
                else:
                    state[4, y, r] = total[y, r] + share * rate
            if n < 3:
                low_copy(n + 1, c).start()
                high_copy(n + 1, c).start()
            else:
                remote, local = result_copy(c)
                mine = (c == me_s) & (home == me_p)

                @pl.when(jnp.logical_not(mine))
                def _():
                    remote.start()

                @pl.when(mine)
                def _():
                    local().start()

    for n in range(4):
        products(n)
        combine(n)

    @pl.when(relays_in)
    def _():
        for k in range(4):
            forward_eddy(k)[1].wait_send()

    @pl.when(crossing)
    def _():
        edge_copy(True).wait_send()

    spread_sent("vel")
    spread_sent("plane")
    spread_sent("eddy")
    row_copy.wait_send()

    @pl.loop(0, 8)
    def _(c):
        for n in range(4):

            @pl.when(low_sends(n, c))
            def _():
                low_copy(n, c).wait_send()

            @pl.when(high_sends(n, c))
            def _():
                high_copy(n, c).wait_send()

        mine = (c == me_s) & (home == me_p)

        @pl.when(jnp.logical_not(mine))
        def _():
            result_copy(c)[0].wait_send()

        pltpu.make_async_copy(
            state.at[4, :, rows8(0)], landed.at[pl.ds(PAIR * c, PAIR)], out_recv.at[c]
        ).wait()
        for y in range(PAIR):
            out_ref[:, pl.ds(PAIR * c + y, 1), :] = jnp.expand_dims(landed[PAIR * c + y], 1)


def ring_shards(
    velocity, eddy_visc, stream_op, inlet_col, planes, record, convection, span_speed, span_filter
):
    span_len = velocity.shape[2]
    half = span_len // 2
    modes = np.arange(half)[:, None]
    angle = (modes * np.arange(span_len)[None, :] % span_len) * (2.0 * np.pi / span_len)
    table = (-2.0 / span_len * modes / half * np.sin(angle)).astype(np.float32)
    f32, dma = jnp.float32, pltpu.SemaphoreType.DMA
    result = pl.pallas_call(
        ring_kernel,
        out_shape=pltpu.VMEM((8, 16, 1024), f32),
        in_specs=[pl.BlockSpec(memory_space=pltpu.HBM)] * 10,
        out_specs=pl.BlockSpec(memory_space=pltpu.VMEM),
        scratch_shapes=[
            pltpu.VMEM((8, 16, 1024), f32),
            pltpu.VMEM((8, 16, 1024), f32),
            pltpu.VMEM((64, 64), f32),
            pltpu.VMEM((1, 64), f32),
            pltpu.VMEM((1, 16, 1024), f32),
            pltpu.SMEM((4,), jnp.int32),
            pltpu.VMEM((1, 16), f32),
            pltpu.VMEM((1, 16), f32),
            pltpu.VMEM((1, 512), f32),
            pltpu.VMEM((512, 1024), f32),
            dma((10,)),
            pltpu.VMEM((64, 128), f32),
            pltpu.VMEM((2, 16, 128), f32),
            pltpu.VMEM((16, 8, 1024), f32),
            pltpu.VMEM((16, 8, 1024), f32),
            pltpu.VMEM((16, 8, 128), f32),
            pltpu.VMEM((5, 2, 64, 1024), f32),
            pltpu.VMEM((2, 64, 1024), f32),
            pltpu.VMEM((8, 2, 8, 128), f32),
            pltpu.VMEM((2, 2, 16, 128), f32),
            pltpu.VMEM((4, 2, 64, 1024), f32),
            pltpu.VMEM((4, 2, 64, 1024), f32),
            pltpu.VMEM((2, 64, 1024), f32),
            pltpu.VMEM((2, 64, 1024), f32),
            pltpu.VMEM((2, 64, 1024), f32),
            pltpu.VMEM((2, 4, 256, 256), jnp.bfloat16),
            pltpu.VMEM((64, 192), jnp.bfloat16),
            dma((8,)), dma((8,)), dma((8,)), dma((8,)), dma((8,)), dma((8,)), dma, dma,
            dma((4, 8)), dma((4, 8)), dma((4, 8)), dma((4, 8)), dma((8,)), dma((8,)),
            pltpu.VMEM((4, 2, 8, 1024), f32), dma((4,)), dma((4,)), dma,
            pltpu.VMEM((16, 8, 1024), f32),
        ],
        compiler_params=pltpu.CompilerParams(
            collective_id=0, has_side_effects=True, vmem_limit_bytes=56 * 2**20
        ),
    )(
        velocity,
        eddy_visc,
        stream_op,
        inlet_col[None, :],
        planes,
        record,
        convection[None, :],
        span_speed[None, :],
        span_filter[None, :],
        jnp.asarray(table),
    )
    return result


def either(velocity, *others):
    fits = (
        lax.axis_size("stream") == 8
        and lax.axis_size("pitch") == 4
        and velocity.shape == (8, 16, 1024)
    )
    return (ring_shards if fits else shards)(velocity, *others)


def solution(mesh):
    placed = (
        P("stream", "pitch", None),
        P("stream", "pitch", None),
        P(),
        P(),
        P("stream", "pitch", None),
        P(),
        P("pitch"),
        P("pitch"),
        P(),
    )
    return jax.shard_map(
        either, mesh=mesh, in_specs=placed, out_specs=P("stream", "pitch", None), check_vma=False
    )
```
